32 devices in a mesh: grp: 2 (over x), gx: 16 (over z, y, core).
Axes of the slice: x: 2, y: 2, z: 4, core: 2. Of those that a mesh axis runs over, the one named last changes fastest.
Arguments:
- pressure_source: float32 [128, 128, 128], P(('grp', 'gx')), parts along dimension 0
- permeability: float32 [128, 128, 128], P(('grp', 'gx')), parts along dimension 0, may hold values from 0.1 to 10
- basis: float32 [40, 128, 128, 128], P(None, ('grp', 'gx')), parts along dimension 1, may hold values from -0.084 to 0.084
- widths: int32 [32], P(('grp', 'gx')), parts along dimension 0, may hold values from 8 to 40, as said below
- extents: int32 [32], P(('grp', 'gx')), parts along dimension 0, may hold values from 1 to 2, as said below
- coarse_owner: int32 [32], P('grp'), parts along dimension 0, may hold values from 0 to 15, as said below
- coarse_inverse: float32 [1280, 640], P(('grp', 'gx')), parts along dimension 0, as said below
Outputs:
- pressure: float32 [128, 128, 128], P(('grp', 'gx')), parts along dimension 0
- residual: float32 [128, 128, 128], P(('grp', 'gx')), parts along dimension 0
The draws below stay inside these ranges and needn't reach their ends.
There are 2 independent parts, one for each index of `grp`. The reference program is written for one: setup_inputs(seed, part) draws one part's arguments, and reference() takes and returns one part's arrays. A program takes and returns all parts, laid end to end along the dimension named above; each array names one. Nothing has to cross between parts.
Inputs may be any that keep to these rules, and one draw needn't show every extreme that they name: `widths`: every draw has a subdomain with 40 vectors and one with 8. `extents`: every draw has a subdomain with 2 margin planes and one with 1. `coarse_owner`: A permutation of the subdomains. `coarse_inverse`: block row b holds the coarse rows of subdomain coarse_owner[b]; the matrix of those rows in subdomain order is symmetric positive definite.
All inputs are finite; a program needn't handle non-finite values.
Results may differ from the reference program's by a relative error of at most 0.0003.
Values sent between devices are 32-bit elements; how exact they have to be, the bound alone decides.
A program may use at most 128 MiB of HBM per device.

```python
import math
import jax
import jax.numpy as jnp
from jax import lax

CX = 4
NY = 128
NZ = 128
KMAX = 40
KMIN = 8
OV = 2
SWEEPS = 6
ITERS = 2
NX = 64
N_GX = 16


def owner_order(key):
    return jax.random.permutation(jax.random.fold_in(key, 101), N_GX).astype(jnp.int32)


def draw_coarse_owner(key, part):
    return owner_order(key)


def draw_coarse_inverse(key, part):
    order = owner_order(key)
    key = jax.random.fold_in(key, 7)
    count = N_GX * KMAX
    noise = jnp.clip(jax.random.normal(jax.random.fold_in(key, 1), (count, count), jnp.float32), -3.0, 3.0)
    spread = 0.42 / math.sqrt(count)
    symmetric = (noise + noise.T) * (0.5 * spread)
    log_high = math.log(3.0)
    diagonal = jnp.exp(jax.random.uniform(jax.random.fold_in(key, 2), (count,), jnp.float32, 0.0, log_high))
    counter = jnp.arange(count, dtype=jnp.int32)
    full = jnp.where(counter[:, None] == counter[None, :], diagonal[:, None], symmetric)
    rows = (order[:, None] * KMAX + jnp.arange(KMAX, dtype=jnp.int32)[None, :]).reshape(-1)
    return full[rows].astype(jnp.float32)


def forced_integers(key, lowest, largest):
    values_out = jax.random.randint(jax.random.fold_in(key, 1), (N_GX,), lowest, largest + 1, dtype=jnp.int32)
    first_slot = jax.random.randint(jax.random.fold_in(key, 2), (), 0, N_GX, dtype=jnp.int32)
    other_slot = (first_slot + jax.random.randint(jax.random.fold_in(key, 3), (), 1, N_GX, dtype=jnp.int32)) % N_GX
    return values_out.at[first_slot].set(largest).at[other_slot].set(lowest)


def draw_widths(key, part):
    key = jax.random.fold_in(key, 11)
    return forced_integers(key, KMIN, KMAX)


def draw_extents(key, part):
    key = jax.random.fold_in(key, 13)
    return forced_integers(key, 1, OV)


def draw_pressure_source(key, part):
    key = jax.random.fold_in(key, 31)
    plane = jnp.arange(NX, dtype=jnp.float32)[:, None, None] / max(NX - 1, 1)
    rough = jnp.clip(jax.random.normal(jax.random.fold_in(key, 1), (NX, NY, NZ), jnp.float32), -4.0, 4.0)
    ramp = jnp.exp(math.log(3.0) * plane)
    return (rough * ramp).astype(jnp.float32)


def shard_levels(stream_key, shape, cuts, low, high):
    factor_of, own = 1.0, jax.random.fold_in(stream_key, 6)
    for dim, parts in cuts:
        draws = jnp.exp(jax.random.uniform(jax.random.fold_in(own, dim), (parts,), jnp.float32, low / len(cuts), high / len(cuts)))
        factor_of = factor_of * jnp.repeat(draws, shape[dim] // parts).reshape([-1 if axis == dim else 1 for axis in range(len(shape))])
    return factor_of


def centred(stream_key, dims, scale, bound, split=(), kind=jnp.bfloat16):
    result = jax.random.normal(stream_key, dims, jnp.float32) * scale
    if len(split) > 0:
        result = shard_levels(stream_key, dims, split, -0.22, 0.18) * result
    return jnp.clip(result, min=-bound, max=bound).astype(kind)


def setup_inputs(seed: int = 0, part: int = 0) -> dict:
    key_list = jax.random.split(jax.random.key(seed), 8)
    part_splits = jax.random.split(jax.random.fold_in(key_list[7], part), 8)
    return {
        "pressure_source": draw_pressure_source(jax.random.fold_in(jax.random.fold_in(key_list[7], part), 71), part),
        "permeability": jnp.clip(jnp.exp(math.log(10.0) - 4.6051702 * jax.random.uniform(part_splits[1], (NX, NY, NZ), jnp.float32) ** shard_levels(part_splits[1], (NX, NY, NZ), ((0, 16),), -0.2, 0.2)), 0.1, 10.0),
        "basis": centred(part_splits[2], (KMAX, NX, NY, NZ), 0.014, 0.084, ((1, 16),), jnp.float32),
        "widths": draw_widths(jax.random.fold_in(jax.random.fold_in(key_list[7], part), 71), part),
        "extents": draw_extents(jax.random.fold_in(jax.random.fold_in(key_list[7], part), 71), part),
        "coarse_owner": draw_coarse_owner(jax.random.fold_in(jax.random.fold_in(key_list[7], part), 71), part),
        "coarse_inverse": draw_coarse_inverse(jax.random.fold_in(jax.random.fold_in(key_list[7], part), 71), part),
    }


OMEGA = 0.8
highest = lax.Precision.HIGHEST


def harmonic(left, right):
    return 2.0 * left * right / (left + right)


def coefficients(padded):
    centre = padded[1:-1, 1:-1, 1:-1]
    lower_x = harmonic(centre, padded[:-2, 1:-1, 1:-1])
    upper_x = harmonic(centre, padded[2:, 1:-1, 1:-1])
    lower_y = harmonic(centre, padded[1:-1, :-2, 1:-1])
    upper_y = harmonic(centre, padded[1:-1, 2:, 1:-1])
    lower_z = harmonic(centre, padded[1:-1, 1:-1, :-2])
    upper_z = harmonic(centre, padded[1:-1, 1:-1, 2:])
    diagonal = lower_x + upper_x + lower_y + upper_y + lower_z + upper_z
    return (lower_x, upper_x, lower_y, upper_y, lower_z, upper_z, diagonal)


def stencil(padded, couplings):
    centre = padded[1:-1, 1:-1, 1:-1]
    beside = couplings[0] * padded[:-2, 1:-1, 1:-1] + couplings[1] * padded[2:, 1:-1, 1:-1]
    beside = beside + couplings[2] * padded[1:-1, :-2, 1:-1] + couplings[3] * padded[1:-1, 2:, 1:-1]
    beside = beside + couplings[4] * padded[1:-1, 1:-1, :-2] + couplings[5] * padded[1:-1, 1:-1, 2:]
    return couplings[6] * centre - beside


def smoother(rhs_values, couplings, inside):
    rhs_values = jnp.where(inside, rhs_values, 0.0)
    update = jnp.zeros_like(rhs_values)
    for sweep in range(SWEEPS):
        action = stencil(jnp.pad(update, 1), couplings)
        update = jnp.where(inside, update + OMEGA * (rhs_values - action) / couplings[6], 0.0)
    return update


def reference(pressure_source, permeability, basis, widths, extents, coarse_owner, coarse_inverse):
    planes = CX + 2 * OV
    own_couplings = coefficients(jnp.pad(permeability, 1, mode="edge"))
    wide_couplings = coefficients(jnp.pad(permeability, ((OV + 1, OV + 1), (1, 1), (1, 1)), mode="edge"))
    column_mask = (jnp.arange(KMAX, dtype=jnp.int32)[None, :] < widths[:, None]).astype(jnp.float32)
    selector = (coarse_owner[None, :] == jnp.arange(N_GX, dtype=jnp.int32)[:, None]).astype(jnp.float32)
    basis_rows = basis.reshape(KMAX, N_GX, CX * NY * NZ)

    def operator(values_in):
        return stencil(jnp.pad(values_in, 1), own_couplings)

    def precondition(residual_in):
        padded = jnp.pad(residual_in, ((OV, OV), (0, 0), (0, 0)))

        def one_domain(accumulated, index):
            first_plane = index * CX
            local_rhs = lax.dynamic_slice_in_dim(padded, first_plane, planes, 0)
            local_couplings = tuple(lax.dynamic_slice_in_dim(component, first_plane, planes, 0) for component in wide_couplings)
            global_plane = first_plane - OV + jnp.arange(planes, dtype=jnp.int32)
            extent = extents[index]
            inside = (global_plane >= first_plane - extent) & (global_plane < first_plane + CX + extent)
            inside = inside & (global_plane >= 0) & (global_plane < NX)
            update = smoother(local_rhs, local_couplings, inside[:, None, None])
            current = lax.dynamic_slice_in_dim(accumulated, first_plane, planes, 0)
            return lax.dynamic_update_slice_in_dim(accumulated, current + update, first_plane, 0), None

        accumulated, unused = lax.scan(one_domain, jnp.zeros(padded.shape, jnp.float32), jnp.arange(N_GX, dtype=jnp.int32))
        local_part = accumulated[OV:OV + NX]
        projected = jnp.einsum("kgn,gn->gk", basis_rows, residual_in.reshape(N_GX, CX * NY * NZ), precision=highest) * column_mask
        solved = jnp.dot(coarse_inverse, projected.reshape(N_GX * KMAX), precision=highest).reshape(N_GX, KMAX)
        coarse = jnp.dot(selector, solved, precision=highest) * column_mask
        correction = jnp.einsum("kgn,gk->gn", basis_rows, coarse, precision=highest).reshape(NX, NY, NZ)
        return local_part + correction

    pressure = jnp.zeros_like(pressure_source)
    residual = pressure_source
    preconditioned = precondition(residual)
    direction = preconditioned
    product_now = jnp.sum(residual * preconditioned)
    for iteration in range(ITERS):
        image = operator(direction)
        step_length = product_now / jnp.sum(direction * image)
        pressure = pressure + step_length * direction
        residual = residual - step_length * image
        if iteration + 1 < ITERS:
            preconditioned = precondition(residual)
            product_next = jnp.sum(residual * preconditioned)
            direction = preconditioned + (product_next / product_now) * direction
            product_now = product_next
    return pressure, residual
```

```python
import functools

import jax
import jax.numpy as jnp
from jax import lax
from jax.experimental import pallas as pl
from jax.experimental.pallas import tpu as pltpu
from jax.sharding import PartitionSpec as P

OV = 2
SWEEPS = 6
OMEGA = 0.8
PAD = 8
ROWS = 32
HALF = 64
GROUP = 8
HIGHEST = lax.Precision.HIGHEST
MESH = pl.DeviceIdType.MESH
F32 = jnp.float32
PERM, RHS, SPILL0, NEAR0, FAR0, SPILL1, NEAR1 = range(7)


def kernel(
    n, src_ref, perm_ref, width_ref, extent_ref, owner_ref, inverse_ref, basis_ref,
    pressure_ref, residual_ref,
    basis, kx, fx, vx, weights, scale, diagonal, rhs, fields, spills, zx, z1x, image,
    rows, coarse_rows, spread, cast, basis_sem, send_sem, recv_sem, cast_send, cast_recv,
):
    me = lax.axis_index("gx")
    own, ny, nz = src_ref.shape
    wide = own + 2 * OV
    modes = basis_ref.shape[0]
    groups = modes // GROUP

    def basis_copy(g):
        part = pl.ds(g * GROUP, GROUP)
        return pltpu.make_async_copy(basis_ref.at[part], basis.at[part], basis_sem.at[g])

    for g in range(groups):
        basis_copy(g).start()

    barrier = pltpu.get_barrier_semaphore()

    @pl.loop(1, n)
    def _(k):
        pl.semaphore_signal(
            barrier, inc=1, device_id={"gx": lax.rem(me + k, n)}, device_id_type=MESH
        )

    pl.semaphore_wait(barrier, n - 1)

    body = pl.ds(PAD, ny)
    plans = {
        PERM: (
            perm_ref.at[pl.ds(0, OV + 1)], kx.at[pl.ds(own + OV + 1, OV + 1)],
            perm_ref.at[pl.ds(own - OV - 1, OV + 1)], kx.at[pl.ds(0, OV + 1)],
        ),
        RHS: (
            src_ref.at[pl.ds(0, OV)], fx.at[pl.ds(own + OV, OV)],
            src_ref.at[pl.ds(own - OV, OV)], fx.at[pl.ds(0, OV)],
        ),
        NEAR0: (
            zx.at[OV + 1, body], zx.at[own + OV + 1, body],
            zx.at[own + OV, body], zx.at[OV, body],
        ),
        FAR0: (
            zx.at[pl.ds(OV + 2, OV), body], zx.at[pl.ds(own + OV + 2, OV), body],
            zx.at[pl.ds(own, OV), body], zx.at[pl.ds(0, OV), body],
        ),
        NEAR1: (
            z1x.at[1, body], z1x.at[own + 1, body],
            z1x.at[own, body], z1x.at[0, body],
        ),
    }
    for call, key in enumerate((SPILL0, SPILL1)):
        plans[key] = (
            fields.at[1, pl.ds(1, OV), body], spills.at[call, 1],
            fields.at[1, pl.ds(own + OV + 1, OV), body], spills.at[call, 0],
        )

    def remote(key, side):
        peer = me - 1 if side == 0 else me + 1
        return pltpu.make_async_remote_copy(
            src_ref=plans[key][2 * side], dst_ref=plans[key][2 * side + 1],
            send_sem=send_sem.at[key, side], recv_sem=recv_sem.at[key, side],
            device_id={"gx": peer}, device_id_type=MESH,
        )

    has_left, has_right = me > 0, me < n - 1

    def send(key):
        @pl.when(has_left)
        def _():
            remote(key, 0).start()

        @pl.when(has_right)
        def _():
            remote(key, 1).start()

    def received(key):
        @pl.when(has_right)
        def _():
            remote(key, 0).wait_recv()

        @pl.when(has_left)
        def _():
            remote(key, 1).wait_recv()

    def sent(key):
        @pl.when(has_left)
        def _():
            remote(key, 0).wait_send()

        @pl.when(has_right)
        def _():
            remote(key, 1).wait_send()

    def broadcast(slot, row):
        cast[slot, me] = row

        @pl.loop(1, n)
        def _(k):
            pltpu.make_async_remote_copy(
                src_ref=cast.at[slot, me], dst_ref=cast.at[slot, me],
                send_sem=cast_send.at[slot], recv_sem=cast_recv.at[slot],
                device_id={"gx": lax.rem(me + k, n)}, device_id_type=MESH,
            ).start()

    def gathered(slot):
        others = cast.at[slot, pl.ds(0, n - 1)]
        pltpu.make_async_copy(others, others, cast_recv.at[slot]).wait()

    def cast_sent(slot):
        others = cast.at[slot, pl.ds(0, n - 1)]
        pltpu.make_async_copy(others, others, cast_send.at[slot]).wait()

    send(PERM)
    send(RHS)

    def clear(ref, planes):
        zero = jnp.zeros((PAD, nz), F32)
        for plane in range(planes):
            ref[plane, pl.ds(0, PAD), :] = zero
            ref[plane, pl.ds(PAD + ny, PAD), :] = zero

    for half in range(2):
        clear(fields.at[half], wide + 2)
        for plane in (0, wide + 1):
            fields[half, plane, body, :] = jnp.zeros((ny, nz), F32)
    clear(zx, own + 2 * OV + 2)
    clear(z1x, own + 2)
    rows[...] = jnp.zeros(rows.shape, F32)
    kx[pl.ds(OV + 1, own)] = perm_ref[...]
    fx[pl.ds(OV, own)] = src_ref[...]

    @pl.when(jnp.logical_not(has_left))
    def _():
        for plane in range(OV + 1):
            kx[plane] = perm_ref[0]
            zx[plane, body, :] = jnp.zeros((ny, nz), F32)
        fx[pl.ds(0, OV)] = jnp.zeros((OV, ny, nz), F32)
        z1x[0, body, :] = jnp.zeros((ny, nz), F32)
        for call in range(2):
            spills[call, 0] = jnp.zeros((OV, ny, nz), F32)

    @pl.when(jnp.logical_not(has_right))
    def _():
        for plane in range(OV + 1):
            kx[own + OV + 1 + plane] = perm_ref[own - 1]
            zx[own + OV + 1 + plane, body, :] = jnp.zeros((ny, nz), F32)
        fx[pl.ds(own + OV, OV)] = jnp.zeros((OV, ny, nz), F32)
        z1x[own + 1, body, :] = jnp.zeros((ny, nz), F32)
        for call in range(2):
            spills[call, 1] = jnp.zeros((OV, ny, nz), F32)

    for i in range(n):
        block = inverse_ref[:, i * modes:(i + 1) * modes]
        coarse_rows[i] = jnp.concatenate(
            [block, jnp.zeros((modes, nz - modes), F32)], axis=1
        )

    width = width_ref[0]
    extent = extent_ref[0]
    lane = lax.broadcasted_iota(jnp.int32, (1, nz), 1)

    def fold(block):
        return jnp.sum(block.reshape(-1, 8, nz), axis=0)

    def to_row(table):
        ones = jnp.ones((8, nz), F32)
        out = lax.dot_general(
            ones, table, (((1,), (1,)), ((), ())), precision=HIGHEST,
            preferred_element_type=F32,
        )
        return out[0:1]

    def project(f_ref, wait):
        halves = ny // HALF

        @pl.loop(0, groups)
        def _(g):
            if wait:
                basis_copy(g).wait()
            base = g * GROUP

            def step(t, sums):
                plane, start = t // halves, pl.multiple_of((t % halves) * HALF, HALF)
                values = f_ref[OV + plane, pl.ds(start, HALF), :]
                return tuple(
                    sums[j] + fold(basis[base + j, plane, pl.ds(start, HALF), :] * values)
                    for j in range(GROUP)
                )

            sums = lax.fori_loop(
                0, own * halves, step, tuple(jnp.zeros((8, nz), F32) for _ in range(GROUP))
            )
            rows[pl.ds(pl.multiple_of(base, GROUP), GROUP), :] = jnp.concatenate(
                [jnp.sum(s, axis=0, keepdims=True) for s in sums], axis=0
            )

        return jnp.where(lane < width, to_row(rows[...]), 0.0)

    def coarse_solve(slot):
        gathered(slot)

        def step(i, total):
            return total + coarse_rows[i] * cast[slot, i]

        table = lax.fori_loop(0, n, step, jnp.zeros((modes, nz), F32))
        table = jnp.concatenate([table, jnp.zeros((nz - modes, nz), F32)], axis=0)
        broadcast(slot + 1, to_row(table))

    def coarse_spread(slot):
        gathered(slot)

        def step(b, total):
            return total + jnp.where(owner_ref[b] == me, cast[slot, b], 0.0)

        mine = lax.fori_loop(0, n, step, jnp.zeros((1, nz), F32))
        mine = jnp.where(lane < width, mine, 0.0)
        at = lax.broadcasted_iota(jnp.int32, (modes, nz), 0)
        across = lax.broadcasted_iota(jnp.int32, (modes, nz), 1)
        spread[...] = jnp.dot(
            jnp.where(at == across, mine, 0.0), jnp.ones((nz, nz), F32),
            precision=HIGHEST, preferred_element_type=F32,
        )

    def harmonic(left, right):
        return 2.0 * left * right / (left + right)

    def couple(p):
        y_at = lax.broadcasted_iota(jnp.int32, (ny, nz), 0)
        z_at = lax.broadcasted_iota(jnp.int32, (ny, nz), 1)
        centre = kx[p + 1]
        lower_x, upper_x = harmonic(centre, kx[p]), harmonic(centre, kx[p + 2])
        upper_y = jnp.where(
            y_at == ny - 1, centre, harmonic(centre, pltpu.roll(centre, ny - 1, 0))
        )
        lower_y = jnp.where(y_at == 0, centre, pltpu.roll(upper_y, 1, 0))
        upper_z = jnp.where(
            z_at == nz - 1, centre, harmonic(centre, pltpu.roll(centre, nz - 1, 1))
        )
        lower_z = jnp.where(z_at == 0, centre, pltpu.roll(upper_z, 1, 1))
        d = lower_x + upper_x + lower_y + upper_y + lower_z + upper_z
        plane = me * own - OV + p
        inside = (p >= OV - extent) & (p < OV + own + extent)
        inside = inside & (plane >= 0) & (plane < n * own)
        factor = jnp.where(inside, OMEGA, 0.0) / d
        diagonal[p] = d * (1.0 / OMEGA)
        scale[p] = factor
        weights[0, p] = lower_x * factor
        weights[1, p] = upper_x * factor
        weights[2, p] = jnp.where(y_at == 0, 0.0, lower_y * factor)
        weights[3, p] = jnp.where(y_at == ny - 1, 0.0, upper_y * factor)
        weights[4, p] = jnp.where(z_at == 0, 0.0, lower_z * factor)
        weights[5, p] = jnp.where(z_at == nz - 1, 0.0, upper_z * factor)

    def beside(ref, q, p, start, centre):
        here, at = pl.ds(start, ROWS), PAD + start
        total = weights[0, p, here, :] * ref[q - 1, pl.ds(at, ROWS), :]
        total += weights[1, p, here, :] * ref[q + 1, pl.ds(at, ROWS), :]
        total += weights[2, p, here, :] * ref[q, pl.ds(at - 1, ROWS), :]
        total += weights[3, p, here, :] * ref[q, pl.ds(at + 1, ROWS), :]
        total += weights[4, p, here, :] * pltpu.roll(centre, 1, 1)
        total += weights[5, p, here, :] * pltpu.roll(centre, nz - 1, 1)
        return total

    def begin(f_ref, p):
        value = f_ref[p] * scale[p]
        rhs[p] = value
        fields[0, p + 1, body, :] = value

    def sweep_plane(source, target, p):
        for start in range(0, ny, ROWS):
            here = pl.ds(PAD + start, ROWS)
            centre = source[p + 1, here, :]
            target[p + 1, here, :] = (
                rhs[p, pl.ds(start, ROWS), :] + (1.0 - OMEGA) * centre
                + beside(source, p + 1, p, start, centre)
            )

    def sweeps(first, last):
        @pl.loop(first, last)
        def _(s):
            source, target = fields.at[s % 2], fields.at[(s + 1) % 2]

            @pl.loop(0, wide)
            def _(p):
                sweep_plane(source, target, p)

    def apply(ref, q, p, start):
        centre = ref[q, pl.ds(PAD + start, ROWS), :]
        near = beside(ref, q, p, start, centre)
        return centre, diagonal[p, pl.ds(start, ROWS), :] * (OMEGA * centre - near)

    def correct(out_ref, first):
        halves = ny // HALF

        @pl.loop(0, own * halves)
        def _(t):
            plane, start = t // halves, pl.multiple_of((t % halves) * HALF, HALF)
            total = fields[1, OV + 1 + plane, pl.ds(PAD + start, HALF), :]
            for j in range(modes):
                total += spread[j:j + 1, :] * basis[j, plane, pl.ds(start, HALF), :]
            out_ref[first + plane, pl.ds(PAD + start, HALF), :] = total

    def precondition(f_ref, slot, key, call, out_ref, first):
        @pl.loop(0, wide)
        def _(p):
            begin(f_ref, p)

        sweeps(0, 2)
        coarse_solve(slot)
        sweeps(2, SWEEPS - 2)
        source, target = fields.at[0], fields.at[1]

        @pl.loop(0, OV)
        def _(p):
            sweep_plane(source, target, p)
            sweep_plane(source, target, p + own + OV)

        send(key)

        @pl.loop(OV, OV + own)
        def _(p):
            sweep_plane(source, target, p)

        coarse_spread(slot + 1)
        correct(out_ref, first)
        received(key)
        for plane in range(OV):
            out_ref[first + plane, body, :] += spills[call, 0, plane]
        for plane in range(OV):
            out_ref[first + own - OV + plane, body, :] += spills[call, 1, plane]

    def total_of(block):
        return jnp.sum(block, axis=(0, 1), keepdims=True)

    zero = jnp.zeros((8, nz), F32)

    broadcast(0, project(fx, True))
    received(PERM)

    @pl.loop(0, wide)
    def _(p):
        couple(p)

    received(RHS)
    precondition(fx, 0, SPILL0, 0, zx, OV + 1)
    send(NEAR0)
    send(FAR0)
    received(NEAR0)

    def first_image(p, sums):
        rz, za = sums
        for start in range(0, ny, ROWS):
            centre, value = apply(zx, p + 1, p, start)
            vx[p, pl.ds(start, ROWS), :] = value
            rz += fold(centre * fx[p, pl.ds(start, ROWS), :])
            za += fold(centre * value)
        return rz, za

    rz, za = lax.fori_loop(OV, OV + own, first_image, (zero, zero))
    row = project(vx, False)
    row = jnp.where(lane == nz - 2, total_of(rz), row)
    row = jnp.where(lane == nz - 1, total_of(za), row)
    broadcast(2, row)
    received(FAR0)

    @pl.loop(0, OV)
    def _(p):
        for q in (p, p + own + OV):
            for start in range(0, ny, ROWS):
                vx[q, pl.ds(start, ROWS), :] = apply(zx, q + 1, q, start)[1]

    sent(SPILL0)
    precondition(vx, 2, SPILL1, 1, z1x, 1)

    sums = lax.fori_loop(0, n, lambda i, s: s + cast[2, i], jnp.zeros((1, nz), F32))
    rz = total_of(jnp.where(lane == nz - 2, sums, 0.0))
    za = total_of(jnp.where(lane == nz - 1, sums, 0.0))
    step0 = rz / za

    @pl.loop(0, own)
    def _(p):
        z1x[p + 1, body, :] = zx[OV + 1 + p, body, :] - step0 * z1x[p + 1, body, :]

    send(NEAR1)
    received(NEAR1)

    def second_image(p, sums):
        rz1, za1, zv = sums
        for start in range(0, ny, ROWS):
            here = pl.ds(start, ROWS)
            centre, value = apply(z1x, p + 1, p + OV, start)
            image[p, here, :] = value
            before = vx[p + OV, here, :]
            rz1 += fold(centre * (fx[p + OV, here, :] - step0 * before))
            za1 += fold(centre * value)
            zv += fold(centre * before)
        return rz1, za1, zv

    rz1, za1, zv = lax.fori_loop(0, own, second_image, (zero, zero, zero))
    row = jnp.where(lane == 0, total_of(rz1), 0.0)
    row = jnp.where(lane == 1, total_of(za1), row)
    row = jnp.where(lane == 2, total_of(zv), row)
    broadcast(4, row)
    gathered(4)
    sums = lax.fori_loop(0, n, lambda i, s: s + cast[4, i], jnp.zeros((1, nz), F32))
    rz1 = total_of(jnp.where(lane == 0, sums, 0.0))
    za1 = total_of(jnp.where(lane == 1, sums, 0.0))
    zv = total_of(jnp.where(lane == 2, sums, 0.0))
    beta = rz1 / rz
    step1 = rz1 / (za1 + beta * (2.0 * zv + beta * za))
    both = step0 + step1 * beta

    @pl.loop(0, own)
    def _(p):
        pressure_ref[p] = both * zx[OV + 1 + p, body, :] + step1 * z1x[p + 1, body, :]
        residual_ref[p] = fx[OV + p] - both * vx[OV + p] - step1 * image[p]

    for key in (PERM, RHS, NEAR0, FAR0, SPILL1, NEAR1):
        sent(key)
    for slot in range(5):
        cast_sent(slot)


def per_device(n, pressure_source, permeability, basis, widths, extents, coarse_owner, coarse_inverse):
    own, ny, nz = pressure_source.shape
    modes = basis.shape[0]
    wide = own + 2 * OV
    tall = ny + 2 * PAD
    vmem = pl.BlockSpec(memory_space=pltpu.VMEM)
    smem = pl.BlockSpec(memory_space=pltpu.SMEM)
    out = jax.ShapeDtypeStruct((own, ny, nz), F32)
    dma = pltpu.SemaphoreType.DMA
    return pl.pallas_call(
        functools.partial(kernel, n),
        out_shape=(out, out),
        in_specs=[vmem, vmem, smem, smem, smem, vmem, pl.BlockSpec(memory_space=pl.ANY)],
        out_specs=(vmem, vmem),
        scratch_shapes=[
            pltpu.VMEM(basis.shape, F32),
            pltpu.VMEM((wide + 2, ny, nz), F32),
            pltpu.VMEM((wide, ny, nz), F32),
            pltpu.VMEM((wide, ny, nz), F32),
            pltpu.VMEM((6, wide, ny, nz), F32),
            pltpu.VMEM((wide, ny, nz), F32),
            pltpu.VMEM((wide, ny, nz), F32),
            pltpu.VMEM((wide, ny, nz), F32),
            pltpu.VMEM((2, wide + 2, tall, nz), F32),
            pltpu.VMEM((2, 2, OV, ny, nz), F32),
            pltpu.VMEM((wide + 2, tall, nz), F32),
            pltpu.VMEM((own + 2, tall, nz), F32),
            pltpu.VMEM((own, ny, nz), F32),
            pltpu.VMEM((nz, nz), F32),
            pltpu.VMEM((n, modes, nz), F32),
            pltpu.VMEM((modes, nz), F32),
            pltpu.VMEM((5, n, 1, nz), F32),
            dma((modes // GROUP,)),
            dma((7, 2)),
            dma((7, 2)),
            dma((5,)),
            dma((5,)),
        ],
        compiler_params=pltpu.CompilerParams(
            collective_id=0, has_side_effects=True, vmem_limit_bytes=48 * 1024 * 1024
        ),
        name="schwarz_cg",
    )(pressure_source, permeability, widths, extents, coarse_owner, coarse_inverse, basis)


def solution(mesh):
    split = P(("grp", "gx"), None, None)
    placed = (
        split, split, P(None, ("grp", "gx"), None, None),
        P(("grp", "gx")), P(("grp", "gx")), P("grp"), P(("grp", "gx"), None),
    )
    return jax.shard_map(
        functools.partial(per_device, mesh.shape["gx"]),
        mesh=mesh, in_specs=placed, out_specs=(split, split), check_vma=False,
    )
```

```python
import functools

import jax
import jax.numpy as jnp
from jax import lax
from jax.experimental import pallas as pl
from jax.experimental.pallas import tpu as pltpu
from jax.sharding import PartitionSpec as P

OV = 2
SWEEPS = 6
OMEGA = 0.8
PAD = 8
ROWS = 32
HALF = 64
GROUP = 8
HIGHEST = lax.Precision.HIGHEST
MESH = pl.DeviceIdType.MESH
F32 = jnp.float32
PERM, RHS, SPILL0, NEAR0, FAR0, SPILL1, NEAR1 = range(7)


def kernel(
    n, src_hbm, perm_hbm, width_hbm, extent_hbm, owner_hbm, inverse_hbm, basis_ref,
    pressure_ref, residual_ref,
    basis, kx, fx, vx, weights, scale, diagonal, rhs, fields, spills, zx, z1x, image,
    rows, coarse_rows, spread, cast, kp, fp, flat, inverse_ref,
    width_ref, extent_ref, owner_ref,
    basis_sem, send_sem, recv_sem, cast_send, cast_recv, load_sem,
):
    me = lax.axis_index("gx")
    own, ny, nz = src_hbm.shape
    tall = ny // 8
    wide = own + 2 * OV
    modes = basis_ref.shape[0]
    groups = modes // GROUP

    def basis_copy(g):
        part = pl.ds(g * GROUP, GROUP)
        return pltpu.make_async_copy(basis_ref.at[part], basis.at[part], basis_sem.at[g])

    loads = [
        pltpu.make_async_copy(source, target, load_sem.at[i])
        for i, (source, target) in enumerate((
            (perm_hbm, kx.at[pl.ds(OV + 1, own)]), (src_hbm, fx.at[pl.ds(OV, own)]),
            (width_hbm, width_ref), (extent_hbm, extent_ref), (owner_hbm, owner_ref),
            (inverse_hbm, inverse_ref),
        ))
    ]
    for load in loads:
        load.start()
    for g in range(groups):
        basis_copy(g).start()

    barrier = pltpu.get_barrier_semaphore()

    @pl.loop(1, n)
    def _(k):
        pl.semaphore_signal(
            barrier, inc=1, device_id={"gx": lax.rem(me + k, n)}, device_id_type=MESH
        )

    pl.semaphore_wait(barrier, n - 1)

    body = pl.ds(PAD, ny)
    plans = {
        PERM: (
            kx.at[pl.ds(OV + 1, OV + 1)], kx.at[pl.ds(own + OV + 1, OV + 1)],
            kx.at[pl.ds(own, OV + 1)], kx.at[pl.ds(0, OV + 1)],
        ),
        RHS: (
            fx.at[pl.ds(OV, OV)], fx.at[pl.ds(own + OV, OV)],
            fx.at[pl.ds(own, OV)], fx.at[pl.ds(0, OV)],
        ),
        NEAR0: (
            zx.at[OV + 1, body], zx.at[own + OV + 1, body],
            zx.at[own + OV, body], zx.at[OV, body],
        ),
        FAR0: (
            zx.at[pl.ds(OV + 2, OV), body], zx.at[pl.ds(own + OV + 2, OV), body],
            zx.at[pl.ds(own, OV), body], zx.at[pl.ds(0, OV), body],
        ),
        NEAR1: (
            z1x.at[1, body], z1x.at[own + 1, body],
            z1x.at[own, body], z1x.at[0, body],
        ),
    }
    for call, key in enumerate((SPILL0, SPILL1)):
        plans[key] = (
            fields.at[1, pl.ds(1, OV), body], spills.at[call, 1],
            fields.at[1, pl.ds(own + OV + 1, OV), body], spills.at[call, 0],
        )

    def remote(key, side):
        peer = me - 1 if side == 0 else me + 1
        return pltpu.make_async_remote_copy(
            src_ref=plans[key][2 * side], dst_ref=plans[key][2 * side + 1],
            send_sem=send_sem.at[key, side], recv_sem=recv_sem.at[key, side],
            device_id={"gx": peer}, device_id_type=MESH,
        )

    has_left, has_right = me > 0, me < n - 1

    def send(key):
        @pl.when(has_left)
        def _():
            remote(key, 0).start()

        @pl.when(has_right)
        def _():
            remote(key, 1).start()

    def received(key):
        @pl.when(has_right)
        def _():
            remote(key, 0).wait_recv()

        @pl.when(has_left)
        def _():
            remote(key, 1).wait_recv()

    def sent(key):
        @pl.when(has_left)
        def _():
            remote(key, 0).wait_send()

        @pl.when(has_right)
        def _():
            remote(key, 1).wait_send()

    def broadcast(slot, row):
        cast[slot, me] = row

        @pl.loop(1, n)
        def _(k):
            pltpu.make_async_remote_copy(
                src_ref=cast.at[slot, me], dst_ref=cast.at[slot, me],
                send_sem=cast_send.at[slot], recv_sem=cast_recv.at[slot],
                device_id={"gx": lax.rem(me + k, n)}, device_id_type=MESH,
            ).start()

    def gathered(slot):
        others = cast.at[slot, pl.ds(0, n - 1)]
        pltpu.make_async_copy(others, others, cast_recv.at[slot]).wait()

    def cast_sent(slot):
        others = cast.at[slot, pl.ds(0, n - 1)]
        pltpu.make_async_copy(others, others, cast_send.at[slot]).wait()

    loads[0].wait()
    send(PERM)
    loads[1].wait()
    send(RHS)

    for half in range(2):
        for plane in (0, wide + 1):
            fields[half, plane, body, :] = jnp.zeros((ny, nz), F32)
    rows[...] = jnp.zeros(rows.shape, F32)

    @pl.when(jnp.logical_not(has_left))
    def _():
        for plane in range(OV + 1):
            kx[plane] = kx[OV + 1]
            zx[plane, body, :] = jnp.zeros((ny, nz), F32)
        fx[pl.ds(0, OV)] = jnp.zeros((OV, ny, nz), F32)
        z1x[0, body, :] = jnp.zeros((ny, nz), F32)
        for call in range(2):
            spills[call, 0] = jnp.zeros((OV, ny, nz), F32)

    @pl.when(jnp.logical_not(has_right))
    def _():
        for plane in range(OV + 1):
            kx[own + OV + 1 + plane] = kx[own + OV]
            zx[own + OV + 1 + plane, body, :] = jnp.zeros((ny, nz), F32)
        fx[pl.ds(own + OV, OV)] = jnp.zeros((OV, ny, nz), F32)
        z1x[own + 1, body, :] = jnp.zeros((ny, nz), F32)
        for call in range(2):
            spills[call, 1] = jnp.zeros((OV, ny, nz), F32)

    for load in loads[2:]:
        load.wait()
    for i in range(n):
        block = inverse_ref[:, i * modes:(i + 1) * modes]
        coarse_rows[i] = jnp.concatenate(
            [block, jnp.zeros((modes, nz - modes), F32)], axis=1
        )

    width = width_ref[0]
    extent = extent_ref[0]
    lane = lax.broadcasted_iota(jnp.int32, (1, nz), 1)

    def fold(block):
        return jnp.sum(block.reshape(-1, 8, nz), axis=0)

    def to_row(table):
        ones = jnp.ones((8, nz), F32)
        out = lax.dot_general(
            ones, table, (((1,), (1,)), ((), ())), precision=HIGHEST,
            preferred_element_type=F32,
        )
        return out[0:1]

    def project(f_ref, first, wait):
        halves = ny // HALF

        @pl.loop(0, groups)
        def _(g):
            if wait:
                basis_copy(g).wait()
            base = g * GROUP

            def step(t, sums):
                plane, start = t // halves, pl.multiple_of((t % halves) * HALF, HALF)
                values = f_ref[first + plane, pl.ds(start, HALF), :]
                return tuple(
                    sums[j] + fold(basis[base + j, plane, pl.ds(start, HALF), :] * values)
                    for j in range(GROUP)
                )

            sums = lax.fori_loop(
                0, own * halves, step, tuple(jnp.zeros((8, nz), F32) for _ in range(GROUP))
            )
            rows[pl.ds(pl.multiple_of(base, GROUP), GROUP), :] = jnp.concatenate(
                [jnp.sum(s, axis=0, keepdims=True) for s in sums], axis=0
            )

        return jnp.where(lane < width, to_row(rows[...]), 0.0)

    def coarse_solve(slot):
        gathered(slot)

        def step(i, total):
            return total + coarse_rows[i] * cast[slot, i]

        table = lax.fori_loop(0, n, step, jnp.zeros((modes, nz), F32))
        table = jnp.concatenate([table, jnp.zeros((nz - modes, nz), F32)], axis=0)
        broadcast(slot + 1, to_row(table))

    def coarse_spread(slot):
        gathered(slot)

        def step(b, total):
            return total + jnp.where(owner_ref[b] == me, cast[slot, b], 0.0)

        mine = lax.fori_loop(0, n, step, jnp.zeros((1, nz), F32))
        mine = jnp.where(lane < width, mine, 0.0)
        at = lax.broadcasted_iota(jnp.int32, (modes, nz), 0)
        across = lax.broadcasted_iota(jnp.int32, (modes, nz), 1)
        spread[...] = jnp.dot(
            jnp.where(at == across, mine, 0.0), jnp.ones((nz, nz), F32),
            precision=HIGHEST, preferred_element_type=F32,
        )

    def harmonic(left, right):
        return 2.0 * left * right / (left + right)

    def reorder(source, q, target, p, first):
        for t in range(tall):
            target[p, pl.ds(first + 8 * t, 8), :] = source[q, pl.ds(t, 8, stride=tall), :]

    def restore(source, q, target, p):
        for t in range(tall):
            target[p, pl.ds(t, 8, stride=tall), :] = source[q, pl.ds(8 * t, 8), :]

    def wrap(ref, q):
        ref[q, pl.ds(0, 8), :] = pltpu.roll(ref[q, pl.ds(PAD + ny - 8, 8), :], 1, 0)
        ref[q, pl.ds(PAD + ny, 8), :] = pltpu.roll(ref[q, pl.ds(PAD, 8), :], 7, 0)

    def order_couplings(p):
        reorder(kx, p, kp, p, PAD)
        at = lax.broadcasted_iota(jnp.int32, (8, nz), 0)
        head, tail = kp[p, pl.ds(PAD, 8), :], kp[p, pl.ds(PAD + ny - 8, 8), :]
        kp[p, pl.ds(0, 8), :] = jnp.where(at == 0, head, pltpu.roll(tail, 1, 0))
        kp[p, pl.ds(PAD + ny, 8), :] = jnp.where(at == 7, tail, pltpu.roll(head, 7, 0))

    def couple(p):
        plane = me * own - OV + p
        inside = (p >= OV - extent) & (p < OV + own + extent)
        inside = inside & (plane >= 0) & (plane < n * own)
        omega = jnp.where(inside, OMEGA, 0.0)
        z_at = lax.broadcasted_iota(jnp.int32, (ROWS, nz), 1)
        for start in range(0, ny, ROWS):
            y_at = start + lax.broadcasted_iota(jnp.int32, (ROWS, nz), 0)
            here, at = pl.ds(start, ROWS), PAD + start
            centre = kp[p + 1, pl.ds(at, ROWS), :]
            lower_x = harmonic(centre, kp[p, pl.ds(at, ROWS), :])
            upper_x = harmonic(centre, kp[p + 2, pl.ds(at, ROWS), :])
            lower_y = harmonic(centre, kp[p + 1, pl.ds(at - 8, ROWS), :])
            upper_y = harmonic(centre, kp[p + 1, pl.ds(at + 8, ROWS), :])
            upper_z = jnp.where(
                z_at == nz - 1, centre, harmonic(centre, pltpu.roll(centre, nz - 1, 1))
            )
            lower_z = jnp.where(z_at == 0, centre, pltpu.roll(upper_z, 1, 1))
            d = lower_x + upper_x + lower_y + upper_y + lower_z + upper_z
            factor = omega / d
            diagonal[p, here, :] = d * (1.0 / OMEGA)
            scale[p, here, :] = factor
            weights[0, p, here, :] = lower_x * factor
            weights[1, p, here, :] = upper_x * factor
            weights[2, p, here, :] = jnp.where(y_at == 0, 0.0, lower_y * factor)
            weights[3, p, here, :] = jnp.where(y_at == ny - 1, 0.0, upper_y * factor)
            weights[4, p, here, :] = jnp.where(z_at == 0, 0.0, lower_z * factor)
            weights[5, p, here, :] = jnp.where(z_at == nz - 1, 0.0, upper_z * factor)

    def beside(ref, q, p, start, centre):
        here, at = pl.ds(start, ROWS), PAD + start
        total = weights[0, p, here, :] * ref[q - 1, pl.ds(at, ROWS), :]
        total += weights[1, p, here, :] * ref[q + 1, pl.ds(at, ROWS), :]
        total += weights[2, p, here, :] * ref[q, pl.ds(at - 8, ROWS), :]
        total += weights[3, p, here, :] * ref[q, pl.ds(at + 8, ROWS), :]
        total += weights[4, p, here, :] * pltpu.roll(centre, 1, 1)
        total += weights[5, p, here, :] * pltpu.roll(centre, nz - 1, 1)
        return total

    def begin(f_ref, p):
        value = f_ref[p] * scale[p]
        rhs[p] = value
        fields[0, p + 1, body, :] = value
        wrap(fields.at[0], p + 1)

    def sweep_plane(source, target, p):
        for start in range(0, ny, ROWS):
            here = pl.ds(PAD + start, ROWS)
            centre = source[p + 1, here, :]
            target[p + 1, here, :] = (
                rhs[p, pl.ds(start, ROWS), :] + (1.0 - OMEGA) * centre
                + beside(source, p + 1, p, start, centre)
            )
        wrap(target, p + 1)

    def sweeps(first, last):
        @pl.loop(first, last)
        def _(s):
            source, target = fields.at[s % 2], fields.at[(s + 1) % 2]

            @pl.loop(0, wide)
            def _(p):
                sweep_plane(source, target, p)

    def apply(ref, q, p, start):
        centre = ref[q, pl.ds(PAD + start, ROWS), :]
        near = beside(ref, q, p, start, centre)
        return centre, diagonal[p, pl.ds(start, ROWS), :] * (OMEGA * centre - near)

    def correct():
        halves = ny // HALF

        @pl.loop(0, own * halves)
        def _(t):
            plane, start = t // halves, pl.multiple_of((t % halves) * HALF, HALF)
            total = jnp.zeros((HALF, nz), F32)
            for j in range(modes):
                total += spread[j:j + 1, :] * basis[j, plane, pl.ds(start, HALF), :]
            flat[plane, pl.ds(start, HALF), :] = total

    def gather_parts(call, out_ref, first):
        for plane in range(own):
            for t in range(tall):
                here = pl.ds(8 * t, 8)
                total = fields[1, OV + 1 + plane, pl.ds(PAD + 8 * t, 8), :]
                total += flat[plane, pl.ds(t, 8, stride=tall), :]
                if plane < OV:
                    total += spills[call, 0, plane, here, :]
                if plane >= own - OV:
                    total += spills[call, 1, plane - own + OV, here, :]
                out_ref[first + plane, pl.ds(PAD + 8 * t, 8), :] = total

    def precondition(f_ref, slot, key, call, out_ref, first):
        @pl.loop(0, wide)
        def _(p):
            begin(f_ref, p)

        sweeps(0, 2)
        coarse_solve(slot)
        sweeps(2, SWEEPS - 2)
        source, target = fields.at[0], fields.at[1]

        @pl.loop(0, OV)
        def _(p):
            sweep_plane(source, target, p)
            sweep_plane(source, target, p + own + OV)

        send(key)

        @pl.loop(OV, OV + own)
        def _(p):
            sweep_plane(source, target, p)

        coarse_spread(slot + 1)
        correct()
        received(key)
        gather_parts(call, out_ref, first)

    def total_of(block):
        return jnp.sum(block, axis=(0, 1), keepdims=True)

    zero = jnp.zeros((8, nz), F32)

    broadcast(0, project(fx, OV, True))
    received(PERM)

    @pl.loop(0, wide + 2)
    def _(p):
        order_couplings(p)

    @pl.loop(0, wide)
    def _(p):
        couple(p)

    received(RHS)

    @pl.loop(0, wide)
    def _(p):
        reorder(fx, p, fp, p, 0)

    precondition(fp, 0, SPILL0, 0, zx, OV + 1)
    send(NEAR0)
    send(FAR0)
    received(NEAR0)

    @pl.loop(OV, own + OV + 2)
    def _(p):
        wrap(zx, p)

    def first_image(p, sums):
        rz, za = sums
        for start in range(0, ny, ROWS):
            centre, value = apply(zx, p + 1, p, start)
            vx[p, pl.ds(start, ROWS), :] = value
            rz += fold(centre * fp[p, pl.ds(start, ROWS), :])
            za += fold(centre * value)
        restore(vx, p, flat, p - OV)
        return rz, za

    rz, za = lax.fori_loop(OV, OV + own, first_image, (zero, zero))
    row = project(flat, 0, False)
    row = jnp.where(lane == nz - 2, total_of(rz), row)
    row = jnp.where(lane == nz - 1, total_of(za), row)
    broadcast(2, row)
    received(FAR0)

    @pl.loop(0, OV)
    def _(p):
        wrap(zx, p)
        wrap(zx, p + own + OV + 2)

    @pl.loop(0, OV)
    def _(p):
        for q in (p, p + own + OV):
            for start in range(0, ny, ROWS):
                vx[q, pl.ds(start, ROWS), :] = apply(zx, q + 1, q, start)[1]

    sent(SPILL0)
    precondition(vx, 2, SPILL1, 1, z1x, 1)

    sums = lax.fori_loop(0, n, lambda i, s: s + cast[2, i], jnp.zeros((1, nz), F32))
    rz = total_of(jnp.where(lane == nz - 2, sums, 0.0))
    za = total_of(jnp.where(lane == nz - 1, sums, 0.0))
    step0 = rz / za

    @pl.loop(0, own)
    def _(p):
        z1x[p + 1, body, :] = zx[OV + 1 + p, body, :] - step0 * z1x[p + 1, body, :]

    send(NEAR1)
    received(NEAR1)

    @pl.loop(0, own + 2)
    def _(p):
        wrap(z1x, p)

    def second_image(p, sums):
        rz1, za1, zv = sums
        for start in range(0, ny, ROWS):
            here = pl.ds(start, ROWS)
            centre, value = apply(z1x, p + 1, p + OV, start)
            image[p, here, :] = value
            before = vx[p + OV, here, :]
            rz1 += fold(centre * (fp[p + OV, here, :] - step0 * before))
            za1 += fold(centre * value)
            zv += fold(centre * before)
        return rz1, za1, zv

    rz1, za1, zv = lax.fori_loop(0, own, second_image, (zero, zero, zero))
    row = jnp.where(lane == 0, total_of(rz1), 0.0)
    row = jnp.where(lane == 1, total_of(za1), row)
    row = jnp.where(lane == 2, total_of(zv), row)
    broadcast(4, row)
    gathered(4)
    sums = lax.fori_loop(0, n, lambda i, s: s + cast[4, i], jnp.zeros((1, nz), F32))
    rz1 = total_of(jnp.where(lane == 0, sums, 0.0))
    za1 = total_of(jnp.where(lane == 1, sums, 0.0))
    zv = total_of(jnp.where(lane == 2, sums, 0.0))
    beta = rz1 / rz
    step1 = rz1 / (za1 + beta * (2.0 * zv + beta * za))
    both = step0 + step1 * beta

    @pl.loop(0, own)
    def _(p):
        for t in range(tall):
            here, at, place = pl.ds(8 * t, 8), pl.ds(PAD + 8 * t, 8), pl.ds(t, 8, stride=tall)
            pressure_ref[p, place, :] = both * zx[OV + 1 + p, at, :] + step1 * z1x[p + 1, at, :]
            residual_ref[p, place, :] = (
                fp[OV + p, here, :] - both * vx[OV + p, here, :] - step1 * image[p, here, :]
            )

    for key in (PERM, RHS, NEAR0, FAR0, SPILL1, NEAR1):
        sent(key)
    for slot in range(5):
        cast_sent(slot)


def per_device(n, pressure_source, permeability, basis, widths, extents, coarse_owner, coarse_inverse):
    own, ny, nz = pressure_source.shape
    modes = basis.shape[0]
    wide = own + 2 * OV
    tall = ny + 2 * PAD
    vmem = pl.BlockSpec(memory_space=pltpu.VMEM)
    hbm = pl.BlockSpec(memory_space=pl.ANY)
    smem = pltpu.SMEM
    out = jax.ShapeDtypeStruct((own, ny, nz), F32)
    dma = pltpu.SemaphoreType.DMA
    return pl.pallas_call(
        functools.partial(kernel, n),
        out_shape=(out, out),
        in_specs=[hbm] * 7,
        out_specs=(vmem, vmem),
        scratch_shapes=[
            pltpu.VMEM(basis.shape, F32),
            pltpu.VMEM((wide + 2, ny, nz), F32),
            pltpu.VMEM((wide, ny, nz), F32),
            pltpu.VMEM((wide, ny, nz), F32),
            pltpu.VMEM((6, wide, ny, nz), F32),
            pltpu.VMEM((wide, ny, nz), F32),
            pltpu.VMEM((wide, ny, nz), F32),
            pltpu.VMEM((wide, ny, nz), F32),
            pltpu.VMEM((2, wide + 2, tall, nz), F32),
            pltpu.VMEM((2, 2, OV, ny, nz), F32),
            pltpu.VMEM((wide + 2, tall, nz), F32),
            pltpu.VMEM((own + 2, tall, nz), F32),
            pltpu.VMEM((own, ny, nz), F32),
            pltpu.VMEM((nz, nz), F32),
            pltpu.VMEM((n, modes, nz), F32),
            pltpu.VMEM((modes, nz), F32),
            pltpu.VMEM((5, n, 1, nz), F32),
            pltpu.VMEM((wide + 2, tall, nz), F32),
            pltpu.VMEM((wide, ny, nz), F32),
            pltpu.VMEM((own, ny, nz), F32),
            pltpu.VMEM(coarse_inverse.shape, F32),
            smem(widths.shape, jnp.int32),
            smem(extents.shape, jnp.int32),
            smem(coarse_owner.shape, jnp.int32),
            dma((modes // GROUP,)),
            dma((7, 2)),
            dma((7, 2)),
            dma((5,)),
            dma((5,)),
            dma((6,)),
        ],
        compiler_params=pltpu.CompilerParams(
            collective_id=0, has_side_effects=True, vmem_limit_bytes=48 * 1024 * 1024
        ),
        name="schwarz_cg",
    )(pressure_source, permeability, widths, extents, coarse_owner, coarse_inverse, basis)


def solution(mesh):
    split = P(("grp", "gx"), None, None)
    placed = (
        split, split, P(None, ("grp", "gx"), None, None),
        P(("grp", "gx")), P(("grp", "gx")), P("grp"), P(("grp", "gx"), None),
    )
    return jax.shard_map(
        functools.partial(per_device, mesh.shape["gx"]),
        mesh=mesh, in_specs=placed, out_specs=(split, split), check_vma=False,
    )
```

```python
import functools

import jax
import jax.numpy as jnp
from jax import lax
from jax.experimental import pallas as pl
from jax.experimental.pallas import tpu as pltpu
from jax.sharding import PartitionSpec as P

OV = 2
SWEEPS = 6
OMEGA = 0.8
PAD = 8
UNROLL = 4
ROWS = 32
HALF = 64
GROUP = 8
HIGHEST = lax.Precision.HIGHEST
MESH = pl.DeviceIdType.MESH
F32 = jnp.float32
PERM, RHS, SPILL0, NEAR0, FAR0, SPILL1, NEAR1 = range(7)


def kernel(
    n, src_hbm, perm_hbm, width_hbm, extent_hbm, owner_hbm, inverse_hbm, basis_ref,
    pressure_ref, residual_ref,
    basis, kx, fx, vx, weights, scale, diagonal, rhs, even, odd, spills, zx, z1x, image,
    rows, coarse_rows, spread, cast, kp, fp, flat, inverse_ref,
    width_ref, extent_ref, owner_ref,
    basis_sem, send_sem, recv_sem, cast_send, cast_recv, load_sem,
):
    me = lax.axis_index("gx")
    own, ny, nz = src_hbm.shape
    tall = ny // 8
    wide = own + 2 * OV
    modes = basis_ref.shape[0]
    groups = modes // GROUP

    def basis_copy(g):
        part = pl.ds(g * GROUP, GROUP)
        return pltpu.make_async_copy(basis_ref.at[part], basis.at[part], basis_sem.at[g])

    loads = [
        pltpu.make_async_copy(source, target, load_sem.at[i])
        for i, (source, target) in enumerate((
            (perm_hbm, kx.at[pl.ds(OV + 1, own)]), (src_hbm, fx.at[pl.ds(OV, own)]),
            (width_hbm, width_ref), (extent_hbm, extent_ref), (owner_hbm, owner_ref),
            (inverse_hbm, inverse_ref),
        ))
    ]
    for load in loads:
        load.start()
    for g in range(groups):
        basis_copy(g).start()

    barrier = pltpu.get_barrier_semaphore()

    @pl.loop(1, n)
    def _(k):
        pl.semaphore_signal(
            barrier, inc=1, device_id={"gx": lax.rem(me + k, n)}, device_id_type=MESH
        )

    pl.semaphore_wait(barrier, n - 1)

    body = pl.ds(PAD, ny)
    plans = {
        PERM: (
            kx.at[pl.ds(OV + 1, OV + 1)], kx.at[pl.ds(own + OV + 1, OV + 1)],
            kx.at[pl.ds(own, OV + 1)], kx.at[pl.ds(0, OV + 1)],
        ),
        RHS: (
            fx.at[pl.ds(OV, OV)], fx.at[pl.ds(own + OV, OV)],
            fx.at[pl.ds(own, OV)], fx.at[pl.ds(0, OV)],
        ),
        NEAR0: (
            zx.at[OV + 1, body], zx.at[own + OV + 1, body],
            zx.at[own + OV, body], zx.at[OV, body],
        ),
        FAR0: (
            zx.at[pl.ds(OV + 2, OV), body], zx.at[pl.ds(own + OV + 2, OV), body],
            zx.at[pl.ds(own, OV), body], zx.at[pl.ds(0, OV), body],
        ),
        NEAR1: (
            z1x.at[1, body], z1x.at[own + 1, body],
            z1x.at[own, body], z1x.at[0, body],
        ),
    }
    for call, key in enumerate((SPILL0, SPILL1)):
        plans[key] = (
            odd.at[pl.ds(1, OV), body], spills.at[call, 1],
            odd.at[pl.ds(own + OV + 1, OV), body], spills.at[call, 0],
        )

    def remote(key, side):
        peer = me - 1 if side == 0 else me + 1
        return pltpu.make_async_remote_copy(
            src_ref=plans[key][2 * side], dst_ref=plans[key][2 * side + 1],
            send_sem=send_sem.at[key, side], recv_sem=recv_sem.at[key, side],
            device_id={"gx": peer}, device_id_type=MESH,
        )

    has_left, has_right = me > 0, me < n - 1

    def send(key):
        @pl.when(has_left)
        def _():
            remote(key, 0).start()

        @pl.when(has_right)
        def _():
            remote(key, 1).start()

    def received(key):
        @pl.when(has_right)
        def _():
            remote(key, 0).wait_recv()

        @pl.when(has_left)
        def _():
            remote(key, 1).wait_recv()

    def sent(key):
        @pl.when(has_left)
        def _():
            remote(key, 0).wait_send()

        @pl.when(has_right)
        def _():
            remote(key, 1).wait_send()

    def broadcast(slot, row):
        cast[slot, me] = row

        @pl.loop(1, n)
        def _(k):
            pltpu.make_async_remote_copy(
                src_ref=cast.at[slot, me], dst_ref=cast.at[slot, me],
                send_sem=cast_send.at[slot], recv_sem=cast_recv.at[slot],
                device_id={"gx": lax.rem(me + k, n)}, device_id_type=MESH,
            ).start()

    def gathered(slot):
        others = cast.at[slot, pl.ds(0, n - 1)]
        pltpu.make_async_copy(others, others, cast_recv.at[slot]).wait()

    def cast_sent(slot):
        others = cast.at[slot, pl.ds(0, n - 1)]
        pltpu.make_async_copy(others, others, cast_send.at[slot]).wait()

    loads[0].wait()
    send(PERM)
    loads[1].wait()
    send(RHS)

    for half in (even, odd):
        for plane in (0, wide + 1):
            half[plane, body, :] = jnp.zeros((ny, nz), F32)
    rows[...] = jnp.zeros(rows.shape, F32)

    @pl.when(jnp.logical_not(has_left))
    def _():
        for plane in range(OV + 1):
            kx[plane] = kx[OV + 1]
            zx[plane, body, :] = jnp.zeros((ny, nz), F32)
        fx[pl.ds(0, OV)] = jnp.zeros((OV, ny, nz), F32)
        z1x[0, body, :] = jnp.zeros((ny, nz), F32)
        for call in range(2):
            spills[call, 0] = jnp.zeros((OV, ny, nz), F32)

    @pl.when(jnp.logical_not(has_right))
    def _():
        for plane in range(OV + 1):
            kx[own + OV + 1 + plane] = kx[own + OV]
            zx[own + OV + 1 + plane, body, :] = jnp.zeros((ny, nz), F32)
        fx[pl.ds(own + OV, OV)] = jnp.zeros((OV, ny, nz), F32)
        z1x[own + 1, body, :] = jnp.zeros((ny, nz), F32)
        for call in range(2):
            spills[call, 1] = jnp.zeros((OV, ny, nz), F32)

    for load in loads[2:]:
        load.wait()
    for i in range(n):
        block = inverse_ref[:, i * modes:(i + 1) * modes]
        coarse_rows[i] = jnp.concatenate(
            [block, jnp.zeros((modes, nz - modes), F32)], axis=1
        )

    width = width_ref[0]
    extent = extent_ref[0]
    lane = lax.broadcasted_iota(jnp.int32, (1, nz), 1)

    def fold(block):
        return jnp.sum(block.reshape(-1, 8, nz), axis=0)

    def to_row(table):
        ones = jnp.ones((8, nz), F32)
        out = lax.dot_general(
            ones, table, (((1,), (1,)), ((), ())), precision=HIGHEST,
            preferred_element_type=F32,
        )
        return out[0:1]

    def project(f_ref, first, wait):
        halves = ny // HALF

        @pl.loop(0, groups)
        def _(g):
            if wait:
                basis_copy(g).wait()
            base = g * GROUP

            def step(t, sums):
                plane, start = t // halves, pl.multiple_of((t % halves) * HALF, HALF)
                values = f_ref[first + plane, pl.ds(start, HALF), :]
                return tuple(
                    sums[j] + fold(basis[base + j, plane, pl.ds(start, HALF), :] * values)
                    for j in range(GROUP)
                )

            sums = lax.fori_loop(
                0, own * halves, step, tuple(jnp.zeros((8, nz), F32) for _ in range(GROUP))
            )
            rows[pl.ds(pl.multiple_of(base, GROUP), GROUP), :] = jnp.concatenate(
                [jnp.sum(s, axis=0, keepdims=True) for s in sums], axis=0
            )

        return jnp.where(lane < width, to_row(rows[...]), 0.0)

    def coarse_solve(slot):
        gathered(slot)

        def step(i, total):
            return total + coarse_rows[i] * cast[slot, i]

        table = lax.fori_loop(0, n, step, jnp.zeros((modes, nz), F32))
        table = jnp.concatenate([table, jnp.zeros((nz - modes, nz), F32)], axis=0)
        broadcast(slot + 1, to_row(table))

    def coarse_spread(slot):
        gathered(slot)

        def step(b, total):
            return total + jnp.where(owner_ref[b] == me, cast[slot, b], 0.0)

        mine = lax.fori_loop(0, n, step, jnp.zeros((1, nz), F32))
        mine = jnp.where(lane < width, mine, 0.0)
        at = lax.broadcasted_iota(jnp.int32, (modes, nz), 0)
        across = lax.broadcasted_iota(jnp.int32, (modes, nz), 1)
        spread[...] = jnp.dot(
            jnp.where(at == across, mine, 0.0), jnp.ones((nz, nz), F32),
            precision=HIGHEST, preferred_element_type=F32,
        )

    def harmonic(left, right):
        return 2.0 * left * right / (left + right)

    def reorder(source, q, target, p, first):
        for t in range(tall):
            target[p, pl.ds(first + 8 * t, 8), :] = source[q, pl.ds(t, 8, stride=tall), :]

    def restore(source, q, target, p):
        for t in range(tall):
            target[p, pl.ds(t, 8, stride=tall), :] = source[q, pl.ds(8 * t, 8), :]

    def wrap(ref, q):
        ref[q, pl.ds(0, 8), :] = pltpu.roll(ref[q, pl.ds(PAD + ny - 8, 8), :], 1, 0)
        ref[q, pl.ds(PAD + ny, 8), :] = pltpu.roll(ref[q, pl.ds(PAD, 8), :], 7, 0)

    def order_couplings(p):
        reorder(kx, p, kp, p, PAD)
        at = lax.broadcasted_iota(jnp.int32, (8, nz), 0)
        head, tail = kp[p, pl.ds(PAD, 8), :], kp[p, pl.ds(PAD + ny - 8, 8), :]
        kp[p, pl.ds(0, 8), :] = jnp.where(at == 0, head, pltpu.roll(tail, 1, 0))
        kp[p, pl.ds(PAD + ny, 8), :] = jnp.where(at == 7, tail, pltpu.roll(head, 7, 0))

    def couple(p):
        plane = me * own - OV + p
        inside = (p >= OV - extent) & (p < OV + own + extent)
        inside = inside & (plane >= 0) & (plane < n * own)
        omega = jnp.where(inside, OMEGA, 0.0)
        z_at = lax.broadcasted_iota(jnp.int32, (ROWS, nz), 1)
        for start in range(0, ny, ROWS):
            y_at = start + lax.broadcasted_iota(jnp.int32, (ROWS, nz), 0)
            here, at = pl.ds(start, ROWS), PAD + start
            centre = kp[p + 1, pl.ds(at, ROWS), :]
            lower_x = harmonic(centre, kp[p, pl.ds(at, ROWS), :])
            upper_x = harmonic(centre, kp[p + 2, pl.ds(at, ROWS), :])
            lower_y = harmonic(centre, kp[p + 1, pl.ds(at - 8, ROWS), :])
            upper_y = harmonic(centre, kp[p + 1, pl.ds(at + 8, ROWS), :])
            upper_z = jnp.where(
                z_at == nz - 1, centre, harmonic(centre, pltpu.roll(centre, nz - 1, 1))
            )
            lower_z = jnp.where(z_at == 0, centre, pltpu.roll(upper_z, 1, 1))
            d = lower_x + upper_x + lower_y + upper_y + lower_z + upper_z
            factor = omega / d
            diagonal[p, here, :] = d * (1.0 / OMEGA)
            scale[p, here, :] = factor
            weights[0, p, here, :] = lower_x * factor
            weights[1, p, here, :] = upper_x * factor
            weights[2, p, here, :] = jnp.where(y_at == 0, 0.0, lower_y * factor)
            weights[3, p, here, :] = jnp.where(y_at == ny - 1, 0.0, upper_y * factor)
            weights[4, p, here, :] = jnp.where(z_at == 0, 0.0, lower_z * factor)
            weights[5, p, here, :] = jnp.where(z_at == nz - 1, 0.0, upper_z * factor)

    def beside(ref, q, p, start, centre):
        here, at = pl.ds(start, ROWS), PAD + start
        total = weights[0, p, here, :] * ref[q - 1, pl.ds(at, ROWS), :]
        total += weights[1, p, here, :] * ref[q + 1, pl.ds(at, ROWS), :]
        total += weights[2, p, here, :] * ref[q, pl.ds(at - 8, ROWS), :]
        total += weights[3, p, here, :] * ref[q, pl.ds(at + 8, ROWS), :]
        total += weights[4, p, here, :] * pltpu.roll(centre, 1, 1)
        total += weights[5, p, here, :] * pltpu.roll(centre, nz - 1, 1)
        return total

    def begin(f_ref, p):
        value = f_ref[p] * scale[p]
        rhs[p] = value
        even[p + 1, body, :] = value
        even[p + 1, pl.ds(0, 8), :] = pltpu.roll(value[-8:], 1, 0)
        even[p + 1, pl.ds(PAD + ny, 8), :] = pltpu.roll(value[:8], 7, 0)

    def sweep_plane(source, target, p):
        for start in range(0, ny, ROWS):
            here = pl.ds(PAD + start, ROWS)
            centre = source[p + 1, here, :]
            value = (
                rhs[p, pl.ds(start, ROWS), :] + (1.0 - OMEGA) * centre
                + beside(source, p + 1, p, start, centre)
            )
            target[p + 1, here, :] = value
            if start == 0:
                target[p + 1, pl.ds(PAD + ny, 8), :] = pltpu.roll(value[:8], 7, 0)
            if start == ny - ROWS:
                target[p + 1, pl.ds(0, 8), :] = pltpu.roll(value[-8:], 1, 0)

    def sweep(source, target):
        @pl.loop(0, wide, step=UNROLL)
        def _(p):
            for more in range(UNROLL):
                sweep_plane(source, target, p + more)

    def apply(ref, q, p, start):
        centre = ref[q, pl.ds(PAD + start, ROWS), :]
        near = beside(ref, q, p, start, centre)
        return centre, diagonal[p, pl.ds(start, ROWS), :] * (OMEGA * centre - near)

    def correct():
        halves = ny // HALF

        @pl.loop(0, own * halves)
        def _(t):
            plane, start = t // halves, pl.multiple_of((t % halves) * HALF, HALF)
            total = jnp.zeros((HALF, nz), F32)
            for j in range(modes):
                total += spread[j:j + 1, :] * basis[j, plane, pl.ds(start, HALF), :]
            flat[plane, pl.ds(start, HALF), :] = total

    def gather_part(call, out_ref, first, plane):
        for t in range(tall):
            here = pl.ds(8 * t, 8)
            total = odd[OV + 1 + plane, pl.ds(PAD + 8 * t, 8), :]
            total += flat[plane, pl.ds(t, 8, stride=tall), :]
            if plane < OV:
                total += spills[call, 0, plane, here, :]
            if plane >= own - OV:
                total += spills[call, 1, plane - own + OV, here, :]
            out_ref[first + plane, pl.ds(PAD + 8 * t, 8), :] = total

    def precondition(f_ref, slot, key):
        @pl.loop(0, wide, step=UNROLL)
        def _(p):
            for more in range(UNROLL):
                begin(f_ref, p + more)

        sweep(even, odd)
        sweep(odd, even)
        coarse_solve(slot)
        sweep(even, odd)
        sweep(odd, even)
        for p in range(OV):
            sweep_plane(even, odd, p)
            sweep_plane(even, odd, p + own + OV)
        send(key)
        for p in range(OV, OV + own):
            sweep_plane(even, odd, p)
        coarse_spread(slot + 1)
        correct()
        received(key)

    def total_of(block):
        return jnp.sum(block, axis=(0, 1), keepdims=True)

    zero = jnp.zeros((8, nz), F32)

    broadcast(0, project(fx, OV, True))
    received(PERM)

    @pl.loop(0, wide + 2)
    def _(p):
        order_couplings(p)

    @pl.loop(0, wide)
    def _(p):
        couple(p)

    received(RHS)

    @pl.loop(0, wide)
    def _(p):
        reorder(fx, p, fp, p, 0)

    precondition(fp, 0, SPILL0)
    ends, middle = (0, own - 1), range(1, own - 1)
    for plane in ends:
        gather_part(0, zx, OV + 1, plane)
    send(NEAR0)
    for plane in middle:
        gather_part(0, zx, OV + 1, plane)
    send(FAR0)

    def first_image(p, sums):
        rz, za = sums
        for start in range(0, ny, ROWS):
            centre, value = apply(zx, p + 1, p, start)
            vx[p, pl.ds(start, ROWS), :] = value
            rz += fold(centre * fp[p, pl.ds(start, ROWS), :])
            za += fold(centre * value)
        restore(vx, p, flat, p - OV)
        return rz, za

    sums = (zero, zero)
    for plane in range(own):
        wrap(zx, OV + 1 + plane)
    for plane in middle:
        sums = first_image(OV + plane, sums)
    received(NEAR0)
    for plane in ends:
        sums = first_image(OV + plane, sums)
    rz, za = sums
    row = project(flat, 0, False)
    row = jnp.where(lane == nz - 2, total_of(rz), row)
    row = jnp.where(lane == nz - 1, total_of(za), row)
    broadcast(2, row)
    received(FAR0)
    for q in (*range(OV), *range(own + OV, wide)):
        wrap(zx, q + 1)
    for q in (*range(OV), *range(own + OV, wide)):
        for start in range(0, ny, ROWS):
            vx[q, pl.ds(start, ROWS), :] = apply(zx, q + 1, q, start)[1]
    sent(SPILL0)
    precondition(vx, 2, SPILL1)

    sums = lax.fori_loop(0, n, lambda i, s: s + cast[2, i], jnp.zeros((1, nz), F32))
    rz = total_of(jnp.where(lane == nz - 2, sums, 0.0))
    za = total_of(jnp.where(lane == nz - 1, sums, 0.0))
    step0 = rz / za

    def second_direction(plane):
        gather_part(1, z1x, 1, plane)
        z1x[plane + 1, body, :] = (
            zx[OV + 1 + plane, body, :] - step0 * z1x[plane + 1, body, :]
        )

    def second_image(p, sums):
        rz1, za1, zv = sums
        for start in range(0, ny, ROWS):
            here = pl.ds(start, ROWS)
            centre, value = apply(z1x, p + 1, p + OV, start)
            image[p, here, :] = value
            before = vx[p + OV, here, :]
            rz1 += fold(centre * (fp[p + OV, here, :] - step0 * before))
            za1 += fold(centre * value)
            zv += fold(centre * before)
        return rz1, za1, zv

    for plane in ends:
        second_direction(plane)
    send(NEAR1)
    for plane in middle:
        second_direction(plane)
    for plane in range(own):
        wrap(z1x, plane + 1)
    sums = (zero, zero, zero)
    for plane in middle:
        sums = second_image(plane, sums)
    received(NEAR1)
    for plane in ends:
        sums = second_image(plane, sums)
    rz1, za1, zv = sums
    row = jnp.where(lane == 0, total_of(rz1), 0.0)
    row = jnp.where(lane == 1, total_of(za1), row)
    row = jnp.where(lane == 2, total_of(zv), row)
    broadcast(4, row)
    gathered(4)
    sums = lax.fori_loop(0, n, lambda i, s: s + cast[4, i], jnp.zeros((1, nz), F32))
    rz1 = total_of(jnp.where(lane == 0, sums, 0.0))
    za1 = total_of(jnp.where(lane == 1, sums, 0.0))
    zv = total_of(jnp.where(lane == 2, sums, 0.0))
    beta = rz1 / rz
    step1 = rz1 / (za1 + beta * (2.0 * zv + beta * za))
    both = step0 + step1 * beta

    @pl.loop(0, own)
    def _(p):
        for t in range(tall):
            here, at, place = pl.ds(8 * t, 8), pl.ds(PAD + 8 * t, 8), pl.ds(t, 8, stride=tall)
            pressure_ref[p, place, :] = both * zx[OV + 1 + p, at, :] + step1 * z1x[p + 1, at, :]
            residual_ref[p, place, :] = (
                fp[OV + p, here, :] - both * vx[OV + p, here, :] - step1 * image[p, here, :]
            )

    for key in (PERM, RHS, NEAR0, FAR0, SPILL1, NEAR1):
        sent(key)
    for slot in range(5):
        cast_sent(slot)


def per_device(n, pressure_source, permeability, basis, widths, extents, coarse_owner, coarse_inverse):
    own, ny, nz = pressure_source.shape
    modes = basis.shape[0]
    wide = own + 2 * OV
    tall = ny + 2 * PAD
    vmem = pl.BlockSpec(memory_space=pltpu.VMEM)
    hbm = pl.BlockSpec(memory_space=pl.ANY)
    smem = pltpu.SMEM
    out = jax.ShapeDtypeStruct((own, ny, nz), F32)
    dma = pltpu.SemaphoreType.DMA
    return pl.pallas_call(
        functools.partial(kernel, n),
        out_shape=(out, out),
        in_specs=[hbm] * 7,
        out_specs=(vmem, vmem),
        scratch_shapes=[
            pltpu.VMEM(basis.shape, F32),
            pltpu.VMEM((wide + 2, ny, nz), F32),
            pltpu.VMEM((wide, ny, nz), F32),
            pltpu.VMEM((wide, ny, nz), F32),
            pltpu.VMEM((6, wide, ny, nz), F32),
            pltpu.VMEM((wide, ny, nz), F32),
            pltpu.VMEM((wide, ny, nz), F32),
            pltpu.VMEM((wide, ny, nz), F32),
            pltpu.VMEM((wide + 2, tall, nz), F32),
            pltpu.VMEM((wide + 2, tall, nz), F32),
            pltpu.VMEM((2, 2, OV, ny, nz), F32),
            pltpu.VMEM((wide + 2, tall, nz), F32),
            pltpu.VMEM((own + 2, tall, nz), F32),
            pltpu.VMEM((own, ny, nz), F32),
            pltpu.VMEM((nz, nz), F32),
            pltpu.VMEM((n, modes, nz), F32),
            pltpu.VMEM((modes, nz), F32),
            pltpu.VMEM((5, n, 1, nz), F32),
            pltpu.VMEM((wide + 2, tall, nz), F32),
            pltpu.VMEM((wide, ny, nz), F32),
            pltpu.VMEM((own, ny, nz), F32),
            pltpu.VMEM(coarse_inverse.shape, F32),
            smem(widths.shape, jnp.int32),
            smem(extents.shape, jnp.int32),
            smem(coarse_owner.shape, jnp.int32),
            dma((modes // GROUP,)),
            dma((7, 2)),
            dma((7, 2)),
            dma((5,)),
            dma((5,)),
            dma((6,)),
        ],
        compiler_params=pltpu.CompilerParams(
            collective_id=0, has_side_effects=True, vmem_limit_bytes=63 * 1024 * 1024
        ),
        name="schwarz_cg",
    )(pressure_source, permeability, widths, extents, coarse_owner, coarse_inverse, basis)


def solution(mesh):
    split = P(("grp", "gx"), None, None)
    placed = (
        split, split, P(None, ("grp", "gx"), None, None),
        P(("grp", "gx")), P(("grp", "gx")), P("grp"), P(("grp", "gx"), None),
    )
    return jax.shard_map(
        functools.partial(per_device, mesh.shape["gx"]),
        mesh=mesh, in_specs=placed, out_specs=(split, split), check_vma=False,
    )
```

```python
import functools

import jax
import jax.numpy as jnp
from jax import lax
from jax.experimental import pallas as pl
from jax.experimental.pallas import tpu as pltpu
from jax.sharding import PartitionSpec as P

OV = 2
SWEEPS = 6
OMEGA = 0.8
PAD = 8
UNROLL = 4
ROWS = 32
HALF = 64
GROUP = 8
HIGHEST = lax.Precision.HIGHEST
MESH = pl.DeviceIdType.MESH
F32 = jnp.float32
PERM, RHS, SPILL0, NEAR0, FAR0, SPILL1, NEAR1 = range(7)


def kernel(
    n, src_hbm, perm_hbm, width_hbm, extent_hbm, owner_hbm, inverse_hbm, basis_ref,
    pressure_ref, residual_ref,
    basis, kx, fx, vx, weights, scale, diagonal, rhs, even, odd, spills, zx, z1x, image,
    rows, coarse_rows, spread, cast, kp, fp, flat, inverse_ref,
    width_ref, extent_ref, owner_ref,
    basis_sem, send_sem, recv_sem, cast_send, cast_recv, load_sem,
):
    me = lax.axis_index("gx")
    own, ny, nz = src_hbm.shape
    tall = ny // 8
    wide = own + 2 * OV
    modes = basis_ref.shape[0]
    groups = modes // GROUP

    def basis_copy(g):
        part = pl.ds(g * GROUP, GROUP)
        return pltpu.make_async_copy(basis_ref.at[part], basis.at[part], basis_sem.at[g])

    loads = [
        pltpu.make_async_copy(source, target, load_sem.at[i])
        for i, (source, target) in enumerate((
            (perm_hbm, kx.at[pl.ds(OV + 1, own)]), (src_hbm, fx.at[pl.ds(OV, own)]),
            (width_hbm, width_ref), (extent_hbm, extent_ref), (owner_hbm, owner_ref),
            (inverse_hbm, inverse_ref),
        ))
    ]
    for load in loads:
        load.start()
    for g in range(groups):
        basis_copy(g).start()

    barrier = pltpu.get_barrier_semaphore()

    @pl.loop(1, n)
    def _(k):
        pl.semaphore_signal(
            barrier, inc=1, device_id={"gx": lax.rem(me + k, n)}, device_id_type=MESH
        )

    pl.semaphore_wait(barrier, n - 1)

    body = pl.ds(PAD, ny)
    plans = {
        PERM: (
            kx.at[pl.ds(OV + 1, OV + 1)], kx.at[pl.ds(own + OV + 1, OV + 1)],
            kx.at[pl.ds(own, OV + 1)], kx.at[pl.ds(0, OV + 1)],
        ),
        RHS: (
            fx.at[pl.ds(OV, OV)], fx.at[pl.ds(own + OV, OV)],
            fx.at[pl.ds(own, OV)], fx.at[pl.ds(0, OV)],
        ),
        NEAR0: (
            zx.at[OV + 1, body], zx.at[own + OV + 1, body],
            zx.at[own + OV, body], zx.at[OV, body],
        ),
        FAR0: (
            zx.at[pl.ds(OV + 2, OV), body], zx.at[pl.ds(own + OV + 2, OV), body],
            zx.at[pl.ds(own, OV), body], zx.at[pl.ds(0, OV), body],
        ),
        NEAR1: (
            z1x.at[1, body], z1x.at[own + 1, body],
            z1x.at[own, body], z1x.at[0, body],
        ),
    }
    for call, key in enumerate((SPILL0, SPILL1)):
        plans[key] = (
            odd.at[pl.ds(1, OV), body], spills.at[call, 1],
            odd.at[pl.ds(own + OV + 1, OV), body], spills.at[call, 0],
        )

    def remote(key, side):
        peer = me - 1 if side == 0 else me + 1
        return pltpu.make_async_remote_copy(
            src_ref=plans[key][2 * side], dst_ref=plans[key][2 * side + 1],
            send_sem=send_sem.at[key, side], recv_sem=recv_sem.at[key, side],
            device_id={"gx": peer}, device_id_type=MESH,
        )

    has_left, has_right = me > 0, me < n - 1

    def send(key):
        @pl.when(has_left)
        def _():
            remote(key, 0).start()

        @pl.when(has_right)
        def _():
            remote(key, 1).start()

    def received(key):
        @pl.when(has_right)
        def _():
            remote(key, 0).wait_recv()

        @pl.when(has_left)
        def _():
            remote(key, 1).wait_recv()

    def sent(key):
        @pl.when(has_left)
        def _():
            remote(key, 0).wait_send()

        @pl.when(has_right)
        def _():
            remote(key, 1).wait_send()

    def broadcast(slot, row):
        cast[slot, me] = row

        @pl.loop(1, n)
        def _(k):
            pltpu.make_async_remote_copy(
                src_ref=cast.at[slot, me], dst_ref=cast.at[slot, me],
                send_sem=cast_send.at[slot], recv_sem=cast_recv.at[slot],
                device_id={"gx": lax.rem(me + k, n)}, device_id_type=MESH,
            ).start()

    def gathered(slot):
        others = cast.at[slot, pl.ds(0, n - 1)]
        pltpu.make_async_copy(others, others, cast_recv.at[slot]).wait()

    def cast_sent(slot):
        others = cast.at[slot, pl.ds(0, n - 1)]
        pltpu.make_async_copy(others, others, cast_send.at[slot]).wait()

    loads[0].wait()
    send(PERM)
    loads[1].wait()
    send(RHS)

    for half in (even, odd):
        for plane in (0, wide + 1):
            half[plane, body, :] = jnp.zeros((ny, nz), F32)
    rows[...] = jnp.zeros(rows.shape, F32)

    @pl.when(jnp.logical_not(has_left))
    def _():
        for plane in range(OV + 1):
            kx[plane] = kx[OV + 1]
            zx[plane, body, :] = jnp.zeros((ny, nz), F32)
        fx[pl.ds(0, OV)] = jnp.zeros((OV, ny, nz), F32)
        z1x[0, body, :] = jnp.zeros((ny, nz), F32)
        for call in range(2):
            spills[call, 0] = jnp.zeros((OV, ny, nz), F32)

    @pl.when(jnp.logical_not(has_right))
    def _():
        for plane in range(OV + 1):
            kx[own + OV + 1 + plane] = kx[own + OV]
            zx[own + OV + 1 + plane, body, :] = jnp.zeros((ny, nz), F32)
        fx[pl.ds(own + OV, OV)] = jnp.zeros((OV, ny, nz), F32)
        z1x[own + 1, body, :] = jnp.zeros((ny, nz), F32)
        for call in range(2):
            spills[call, 1] = jnp.zeros((OV, ny, nz), F32)

    for load in loads[2:]:
        load.wait()
    for i in range(n):
        block = inverse_ref[:, i * modes:(i + 1) * modes]
        coarse_rows[i] = jnp.concatenate(
            [block, jnp.zeros((modes, nz - modes), F32)], axis=1
        )

    width = width_ref[0]
    extent = extent_ref[0]
    lane = lax.broadcasted_iota(jnp.int32, (1, nz), 1)

    def fold(block):
        return jnp.sum(block.reshape(-1, 8, nz), axis=0)

    def to_row(table):
        ones = jnp.ones((8, nz), F32)
        out = lax.dot_general(
            ones, table, (((1,), (1,)), ((), ())), precision=HIGHEST,
            preferred_element_type=F32,
        )
        return out[0:1]

    def project(f_ref, first, wait):
        halves = ny // HALF

        @pl.loop(0, groups)
        def _(g):
            if wait:
                basis_copy(g).wait()
            base = g * GROUP

            def step(t, sums):
                plane, start = t // halves, pl.multiple_of((t % halves) * HALF, HALF)
                values = f_ref[first + plane, pl.ds(start, HALF), :]
                return tuple(
                    sums[j] + fold(basis[base + j, plane, pl.ds(start, HALF), :] * values)
                    for j in range(GROUP)
                )

            sums = lax.fori_loop(
                0, own * halves, step, tuple(jnp.zeros((8, nz), F32) for _ in range(GROUP))
            )
            rows[pl.ds(pl.multiple_of(base, GROUP), GROUP), :] = jnp.concatenate(
                [jnp.sum(s, axis=0, keepdims=True) for s in sums], axis=0
            )

        return jnp.where(lane < width, to_row(rows[...]), 0.0)

    def coarse_solve(slot):
        gathered(slot)

        def step(i, total):
            return total + coarse_rows[i] * cast[slot, i]

        table = lax.fori_loop(0, n, step, jnp.zeros((modes, nz), F32))
        table = jnp.concatenate([table, jnp.zeros((nz - modes, nz), F32)], axis=0)
        broadcast(slot + 1, to_row(table))

    def coarse_spread(slot):
        gathered(slot)

        def step(b, total):
            return total + jnp.where(owner_ref[b] == me, cast[slot, b], 0.0)

        mine = lax.fori_loop(0, n, step, jnp.zeros((1, nz), F32))
        mine = jnp.where(lane < width, mine, 0.0)
        at = lax.broadcasted_iota(jnp.int32, (modes, nz), 0)
        across = lax.broadcasted_iota(jnp.int32, (modes, nz), 1)
        spread[...] = jnp.dot(
            jnp.where(at == across, mine, 0.0), jnp.ones((nz, nz), F32),
            precision=HIGHEST, preferred_element_type=F32,
        )

    def harmonic(left, right):
        return 2.0 * left * right / (left + right)

    def reorder(source, q, target, p, first):
        for t in range(tall):
            target[p, pl.ds(first + 8 * t, 8), :] = source[q, pl.ds(t, 8, stride=tall), :]

    def restore(source, q, target, p):
        for t in range(tall):
            target[p, pl.ds(t, 8, stride=tall), :] = source[q, pl.ds(8 * t, 8), :]

    def wrap(ref, q):
        ref[q, pl.ds(0, 8), :] = pltpu.roll(ref[q, pl.ds(PAD + ny - 8, 8), :], 1, 0)
        ref[q, pl.ds(PAD + ny, 8), :] = pltpu.roll(ref[q, pl.ds(PAD, 8), :], 7, 0)

    def order_couplings(p):
        reorder(kx, p, kp, p, PAD)
        at = lax.broadcasted_iota(jnp.int32, (8, nz), 0)
        head, tail = kp[p, pl.ds(PAD, 8), :], kp[p, pl.ds(PAD + ny - 8, 8), :]
        kp[p, pl.ds(0, 8), :] = jnp.where(at == 0, head, pltpu.roll(tail, 1, 0))
        kp[p, pl.ds(PAD + ny, 8), :] = jnp.where(at == 7, tail, pltpu.roll(head, 7, 0))

    def couple(p):
        plane = me * own - OV + p
        inside = (p >= OV - extent) & (p < OV + own + extent)
        inside = inside & (plane >= 0) & (plane < n * own)
        omega = jnp.where(inside, OMEGA, 0.0)
        z_at = lax.broadcasted_iota(jnp.int32, (ROWS, nz), 1)
        for start in range(0, ny, ROWS):
            y_at = start + lax.broadcasted_iota(jnp.int32, (ROWS, nz), 0)
            here, at = pl.ds(start, ROWS), PAD + start
            centre = kp[p + 1, pl.ds(at, ROWS), :]
            lower_x = harmonic(centre, kp[p, pl.ds(at, ROWS), :])
            upper_x = harmonic(centre, kp[p + 2, pl.ds(at, ROWS), :])
            lower_y = harmonic(centre, kp[p + 1, pl.ds(at - 8, ROWS), :])
            upper_y = harmonic(centre, kp[p + 1, pl.ds(at + 8, ROWS), :])
            upper_z = jnp.where(
                z_at == nz - 1, centre, harmonic(centre, pltpu.roll(centre, nz - 1, 1))
            )
            lower_z = jnp.where(z_at == 0, centre, pltpu.roll(upper_z, 1, 1))
            d = lower_x + upper_x + lower_y + upper_y + lower_z + upper_z
            factor = omega / d
            diagonal[p, here, :] = d * (1.0 / OMEGA)
            scale[p, here, :] = factor
            weights[0, p, here, :] = lower_x * factor
            weights[1, p, here, :] = upper_x * factor
            weights[2, p, here, :] = jnp.where(y_at == 0, 0.0, lower_y * factor)
            weights[3, p, here, :] = jnp.where(y_at == ny - 1, 0.0, upper_y * factor)
            weights[4, p, here, :] = jnp.where(z_at == 0, 0.0, lower_z * factor)
            weights[5, p, here, :] = jnp.where(z_at == nz - 1, 0.0, upper_z * factor)

    def beside(ref, q, p, start, centre):
        here, at = pl.ds(start, ROWS), PAD + start
        total = weights[0, p, here, :] * ref[q - 1, pl.ds(at, ROWS), :]
        total += weights[1, p, here, :] * ref[q + 1, pl.ds(at, ROWS), :]
        total += weights[2, p, here, :] * ref[q, pl.ds(at - 8, ROWS), :]
        total += weights[3, p, here, :] * ref[q, pl.ds(at + 8, ROWS), :]
        total += weights[4, p, here, :] * pltpu.roll(centre, 1, 1)
        total += weights[5, p, here, :] * pltpu.roll(centre, nz - 1, 1)
        return total

    def begin(f_ref, p):
        value = f_ref[p] * scale[p]
        rhs[p] = value
        even[p + 1, body, :] = value
        even[p + 1, pl.ds(0, 8), :] = pltpu.roll(value[-8:], 1, 0)
        even[p + 1, pl.ds(PAD + ny, 8), :] = pltpu.roll(value[:8], 7, 0)

    def sweep_plane(source, target, p):
        for start in range(0, ny, ROWS):
            here = pl.ds(PAD + start, ROWS)
            centre = source[p + 1, here, :]
            value = (
                rhs[p, pl.ds(start, ROWS), :] + (1.0 - OMEGA) * centre
                + beside(source, p + 1, p, start, centre)
            )
            target[p + 1, here, :] = value
            if start == 0:
                target[p + 1, pl.ds(PAD + ny, 8), :] = pltpu.roll(value[:8], 7, 0)
            if start == ny - ROWS:
                target[p + 1, pl.ds(0, 8), :] = pltpu.roll(value[-8:], 1, 0)

    def sweep(source, target):
        @pl.loop(0, wide, step=UNROLL)
        def _(p):
            for more in range(UNROLL):
                sweep_plane(source, target, p + more)

    def apply(ref, q, p, start):
        centre = ref[q, pl.ds(PAD + start, ROWS), :]
        near = beside(ref, q, p, start, centre)
        return centre, diagonal[p, pl.ds(start, ROWS), :] * (OMEGA * centre - near)

    def correct():
        halves = ny // HALF

        @pl.loop(0, own * halves)
        def _(t):
            plane, start = t // halves, pl.multiple_of((t % halves) * HALF, HALF)
            total = jnp.zeros((HALF, nz), F32)
            for j in range(modes):
                total += spread[j:j + 1, :] * basis[j, plane, pl.ds(start, HALF), :]
            flat[plane, pl.ds(start, HALF), :] = total

    def gather_part(call, out_ref, first, plane):
        for t in range(tall):
            here = pl.ds(8 * t, 8)
            total = odd[OV + 1 + plane, pl.ds(PAD + 8 * t, 8), :]
            total += flat[plane, pl.ds(t, 8, stride=tall), :]
            if plane < OV:
                total += spills[call, 0, plane, here, :]
            if plane >= own - OV:
                total += spills[call, 1, plane - own + OV, here, :]
            out_ref[first + plane, pl.ds(PAD + 8 * t, 8), :] = total

    def precondition(f_ref, slot, key):
        @pl.loop(0, wide, step=UNROLL)
        def _(p):
            for more in range(UNROLL):
                begin(f_ref, p + more)

        sweep(even, odd)
        sweep(odd, even)
        coarse_solve(slot)
        sweep(even, odd)
        sweep(odd, even)
        for p in range(OV):
            sweep_plane(even, odd, p)
            sweep_plane(even, odd, p + own + OV)
        send(key)
        for p in range(OV, OV + own):
            sweep_plane(even, odd, p)
        coarse_spread(slot + 1)
        correct()
        received(key)

    def total_of(block):
        return jnp.sum(block, axis=(0, 1), keepdims=True)

    zero = jnp.zeros((8, nz), F32)

    for p in range(OV + 1, own + OV + 1):
        order_couplings(p)
    for p in range(OV + 1, own + OV - 1):
        couple(p)
    for p in range(OV, own + OV):
        reorder(fx, p, fp, p, 0)
    broadcast(0, project(fx, OV, True))
    received(PERM)

    for p in (*range(OV + 1), *range(own + OV + 1, wide + 2)):
        order_couplings(p)
    for p in (*range(OV + 1), *range(own + OV - 1, wide)):
        couple(p)
    received(RHS)
    for p in (*range(OV), *range(own + OV, wide)):
        reorder(fx, p, fp, p, 0)

    precondition(fp, 0, SPILL0)
    ends, middle = (0, own - 1), range(1, own - 1)
    for plane in ends:
        gather_part(0, zx, OV + 1, plane)
    send(NEAR0)
    for plane in middle:
        gather_part(0, zx, OV + 1, plane)
    send(FAR0)

    def first_image(p, sums):
        rz, za = sums
        for start in range(0, ny, ROWS):
            centre, value = apply(zx, p + 1, p, start)
            vx[p, pl.ds(start, ROWS), :] = value
            rz += fold(centre * fp[p, pl.ds(start, ROWS), :])
            za += fold(centre * value)
        restore(vx, p, flat, p - OV)
        return rz, za

    sums = (zero, zero)
    for plane in range(own):
        wrap(zx, OV + 1 + plane)
    for plane in middle:
        sums = first_image(OV + plane, sums)
    received(NEAR0)
    for plane in ends:
        sums = first_image(OV + plane, sums)
    rz, za = sums
    row = project(flat, 0, False)
    row = jnp.where(lane == nz - 2, total_of(rz), row)
    row = jnp.where(lane == nz - 1, total_of(za), row)
    broadcast(2, row)
    received(FAR0)
    for q in (*range(OV), *range(own + OV, wide)):
        wrap(zx, q + 1)
    for q in (*range(OV), *range(own + OV, wide)):
        for start in range(0, ny, ROWS):
            vx[q, pl.ds(start, ROWS), :] = apply(zx, q + 1, q, start)[1]
    sent(SPILL0)
    precondition(vx, 2, SPILL1)

    sums = lax.fori_loop(0, n, lambda i, s: s + cast[2, i], jnp.zeros((1, nz), F32))
    rz = total_of(jnp.where(lane == nz - 2, sums, 0.0))
    za = total_of(jnp.where(lane == nz - 1, sums, 0.0))
    step0 = rz / za

    def second_direction(plane):
        gather_part(1, z1x, 1, plane)
        z1x[plane + 1, body, :] = (
            zx[OV + 1 + plane, body, :] - step0 * z1x[plane + 1, body, :]
        )

    def second_image(p, sums):
        rz1, za1, zv = sums
        for start in range(0, ny, ROWS):
            here = pl.ds(start, ROWS)
            centre, value = apply(z1x, p + 1, p + OV, start)
            image[p, here, :] = value
            before = vx[p + OV, here, :]
            rz1 += fold(centre * (fp[p + OV, here, :] - step0 * before))
            za1 += fold(centre * value)
            zv += fold(centre * before)
        return rz1, za1, zv

    for plane in ends:
        second_direction(plane)
    send(NEAR1)
    for plane in middle:
        second_direction(plane)
    for plane in range(own):
        wrap(z1x, plane + 1)
    sums = (zero, zero, zero)
    for plane in middle:
        sums = second_image(plane, sums)
    received(NEAR1)
    for plane in ends:
        sums = second_image(plane, sums)
    rz1, za1, zv = sums
    row = jnp.where(lane == 0, total_of(rz1), 0.0)
    row = jnp.where(lane == 1, total_of(za1), row)
    row = jnp.where(lane == 2, total_of(zv), row)
    broadcast(4, row)
    gathered(4)
    sums = lax.fori_loop(0, n, lambda i, s: s + cast[4, i], jnp.zeros((1, nz), F32))
    rz1 = total_of(jnp.where(lane == 0, sums, 0.0))
    za1 = total_of(jnp.where(lane == 1, sums, 0.0))
    zv = total_of(jnp.where(lane == 2, sums, 0.0))
    beta = rz1 / rz
    step1 = rz1 / (za1 + beta * (2.0 * zv + beta * za))
    both = step0 + step1 * beta

    @pl.loop(0, own)
    def _(p):
        for t in range(tall):
            here, at, place = pl.ds(8 * t, 8), pl.ds(PAD + 8 * t, 8), pl.ds(t, 8, stride=tall)
            pressure_ref[p, place, :] = both * zx[OV + 1 + p, at, :] + step1 * z1x[p + 1, at, :]
            residual_ref[p, place, :] = (
                fp[OV + p, here, :] - both * vx[OV + p, here, :] - step1 * image[p, here, :]
            )

    for key in (PERM, RHS, NEAR0, FAR0, SPILL1, NEAR1):
        sent(key)
    for slot in range(5):
        cast_sent(slot)


def per_device(n, pressure_source, permeability, basis, widths, extents, coarse_owner, coarse_inverse):
    own, ny, nz = pressure_source.shape
    modes = basis.shape[0]
    wide = own + 2 * OV
    tall = ny + 2 * PAD
    vmem = pl.BlockSpec(memory_space=pltpu.VMEM)
    hbm = pl.BlockSpec(memory_space=pl.ANY)
    smem = pltpu.SMEM
    out = jax.ShapeDtypeStruct((own, ny, nz), F32)
    dma = pltpu.SemaphoreType.DMA
    return pl.pallas_call(
        functools.partial(kernel, n),
        out_shape=(out, out),
        in_specs=[hbm] * 7,
        out_specs=(vmem, vmem),
        scratch_shapes=[
            pltpu.VMEM(basis.shape, F32),
            pltpu.VMEM((wide + 2, ny, nz), F32),
            pltpu.VMEM((wide, ny, nz), F32),
            pltpu.VMEM((wide, ny, nz), F32),
            pltpu.VMEM((6, wide, ny, nz), F32),
            pltpu.VMEM((wide, ny, nz), F32),
            pltpu.VMEM((wide, ny, nz), F32),
            pltpu.VMEM((wide, ny, nz), F32),
            pltpu.VMEM((wide + 2, tall, nz), F32),
            pltpu.VMEM((wide + 2, tall, nz), F32),
            pltpu.VMEM((2, 2, OV, ny, nz), F32),
            pltpu.VMEM((wide + 2, tall, nz), F32),
            pltpu.VMEM((own + 2, tall, nz), F32),
            pltpu.VMEM((own, ny, nz), F32),
            pltpu.VMEM((nz, nz), F32),
            pltpu.VMEM((n, modes, nz), F32),
            pltpu.VMEM((modes, nz), F32),
            pltpu.VMEM((5, n, 1, nz), F32),
            pltpu.VMEM((wide + 2, tall, nz), F32),
            pltpu.VMEM((wide, ny, nz), F32),
            pltpu.VMEM((own, ny, nz), F32),
            pltpu.VMEM(coarse_inverse.shape, F32),
            smem(widths.shape, jnp.int32),
            smem(extents.shape, jnp.int32),
            smem(coarse_owner.shape, jnp.int32),
            dma((modes // GROUP,)),
            dma((7, 2)),
            dma((7, 2)),
            dma((5,)),
            dma((5,)),
            dma((6,)),
        ],
        compiler_params=pltpu.CompilerParams(
            collective_id=0, has_side_effects=True, vmem_limit_bytes=63 * 1024 * 1024
        ),
        name="schwarz_cg",
    )(pressure_source, permeability, widths, extents, coarse_owner, coarse_inverse, basis)


def solution(mesh):
    split = P(("grp", "gx"), None, None)
    placed = (
        split, split, P(None, ("grp", "gx"), None, None),
        P(("grp", "gx")), P(("grp", "gx")), P("grp"), P(("grp", "gx"), None),
    )
    return jax.shard_map(
        functools.partial(per_device, mesh.shape["gx"]),
        mesh=mesh, in_specs=placed, out_specs=(split, split), check_vma=False,
    )
```
